32 devices in a mesh: groups: 2 (over x), family: 16 (over z, y, core).
Axes of the slice: x: 2, y: 2, z: 4, core: 2. Of those that a mesh axis runs over, the one named last changes fastest.
Arguments:
- fraction: float32 [128, 32, 32, 128], P(('groups', 'family')), parts along dimension 0, may hold values from 0 to 1
- fraction_start: float32 [128, 32, 32, 128], P(('groups', 'family')), parts along dimension 0, may hold values from 0 to 1
- velocity: bfloat16 [128, 3, 32, 32, 128], P(('groups', 'family')), parts along dimension 0, may hold values from -12 to 12
- interface_flags: int32 [128, 32, 32, 128], P(('groups', 'family')), parts along dimension 0, may hold values 0 or 1
- block_links: int32 [64, 4, 3], P('family'), may hold values from 0 to 63, as said below
- deck_node: int32 [64, 32, 32], P('family'), may hold values from 0 to 2047
- mode_shapes: float32 [40, 2048], replicated, may hold values from -4 to 4
- mobility: float32 [40], replicated, may hold values from 0.3 to 3
Outputs:
- updated_fraction: float32 [128, 32, 32, 128], P(('groups', 'family')), parts along dimension 0
- deck_speed: float32 [128, 32, 32], P(('groups', 'family')), parts along dimension 0
The draws below stay inside these ranges and needn't reach their ends.
There are 2 independent parts, one for each index of `groups`. The reference program is written for one: setup_inputs(seed, part) draws one part's arguments, and reference() takes and returns one part's arrays. A program takes and returns all parts, laid end to end along the dimension named above; an argument that names none is the same for every part. Nothing has to cross between parts.
Inputs may be any that keep to these rules, and one draw needn't show every extreme that they name: `block_links`: every lateral face is matched with exactly one face of a block on another device, both ways with the same flip code. The blocks of device d (blocks d * 4 to (d + 1) * 4 - 1) have their partners on 4 partner devices, each sharing exactly 4 matched face pairs with d; every partner device's index differs from d's in exactly one bit, a different bit for each partner. Faces are matched in no particular order. Entries are partner block, partner face 0 to 3, flip 0 or 1.
All inputs are finite; a program needn't handle non-finite values. Where the reference program divides by a largest or mean magnitude, that divisor is 1e-20 or more. No bound on the sum of `interface_flags` on one device may be relied on, other than what follows from the above.
Results may differ from the reference program's by a relative error of at most 0.0003.
Values sent between devices are 32-bit elements; how exact they have to be, the bound alone decides.
No kernel may reach another device: no remote copies, remote signals or barrier semaphores. Data moves between devices by JAX's collectives and lax.ppermute only.
A program may use at most 256 MiB of HBM per device.

```python
import math
import jax
import jax.numpy as jnp
from jax import lax

SIDE = 32
HEIGHT = 128
BLK_DEV = 4
CAP = 4
NODES = 2048
MODES = 40
BLOCKS = 64
N_FAMILY = 16


def draw_velocity(key, part):
    key = jax.random.fold_in(key, 9)
    key_scale, key_base = jax.random.split(key)
    shape = (BLOCKS, 3, SIDE, SIDE, HEIGHT)
    scales = jnp.exp(jax.random.uniform(key_scale, (BLOCKS, 1, 1, 1, 1), jnp.float32, math.log(0.3), math.log(3.0)))
    base = jnp.clip(jax.random.normal(key_base, shape, jnp.float32), -4.0, 4.0)
    return (scales * base).astype(jnp.bfloat16)


def shuffle_faces(subkey):
    return jax.random.permutation(subkey, 4 * BLK_DEV).astype(jnp.int32)


def draw_block_links(key, part):
    key = jax.random.fold_in(key, 5)
    key_shift, key_order, key_flip = jax.random.split(key, 3)
    face_total = 4 * BLK_DEV
    bit_count = N_FAMILY.bit_length() - 1
    offset = jax.random.randint(key_shift, (), 0, bit_count)
    rounds = jnp.arange(face_total, dtype=jnp.int32)
    round_bits = ((rounds // CAP + offset) % bit_count).astype(jnp.int32)
    round_masks = jnp.left_shift(jnp.ones_like(round_bits), round_bits)
    face_order = jax.vmap(shuffle_faces)(jax.random.split(key_order, N_FAMILY))
    flip_codes = jax.random.randint(key_flip, (N_FAMILY, face_total), 0, 2).astype(jnp.int32)
    device_index = jnp.arange(N_FAMILY, dtype=jnp.int32)[:, None]
    peer_dev = jnp.bitwise_xor(device_index, round_masks[None, :])
    partner_slot = face_order[peer_dev, rounds[None, :]]
    partner_block = peer_dev * BLK_DEV + partner_slot // 4
    flipped = flip_codes[jnp.minimum(device_index, peer_dev), rounds[None, :]]
    row_index = (device_index * BLK_DEV + face_order // 4).reshape(-1)
    col_index = (face_order % 4).reshape(-1)
    link_table = jnp.stack([partner_block, partner_slot % 4, flipped], -1).reshape(-1, 3).astype(jnp.int32)
    return jnp.zeros((BLOCKS, 4, 3), jnp.int32).at[row_index, col_index].set(link_table)


def touch_ends(result, own_key, least, top_value):
    longest = result.shape.index(max(result.shape))
    spots = []
    for shift in (0, 1):
        where = [jax.random.randint(jax.random.fold_in(own_key, axis), (), 0, length) for axis, length in enumerate(result.shape)]
        where[longest] = (where[longest] + shift) % result.shape[longest]
        spots.append(tuple(where))
    return result.at[spots[0]].set(least).at[spots[1]].set(top_value)


def block_scale(stream_key, dims, cuts, least, largest):
    def one(dim, shards_of):
        heights = jax.random.uniform(jax.random.fold_in(jax.random.fold_in(stream_key, 6), dim), (shards_of,), jnp.float32, least / len(cuts), largest / len(cuts))
        return jnp.repeat(jnp.exp(heights), dims[dim] // shards_of).reshape((-1,) + (1,) * (len(dims) - dim - 1))

    factor_of = one(*cuts[0])
    for cut in cuts[1:]:
        factor_of = factor_of * one(*cut)
    return factor_of


def centred(key, shape, spread, most, kind=jnp.bfloat16):
    result = jax.random.normal(key, shape, jnp.float32) * spread
    return jnp.minimum(jnp.maximum(result, -most), most).astype(kind)


def setup_inputs(seed: int = 0, part: int = 0) -> dict:
    streams_of = jax.random.split(jax.random.key(seed), 9)
    part_keys = jax.random.split(jax.random.fold_in(streams_of[8], part), 9)
    fraction = jnp.clip(1.0 * jax.random.uniform(part_keys[0], (BLOCKS, SIDE, SIDE, HEIGHT), jnp.float32) ** block_scale(part_keys[0], (BLOCKS, SIDE, SIDE, HEIGHT), ((0, 16),), -0.2, 0.2), 0.0, 1.0)
    fraction_start = jnp.clip(1.0 * jax.random.uniform(part_keys[1], (BLOCKS, SIDE, SIDE, HEIGHT), jnp.float32) ** block_scale(part_keys[1], (BLOCKS, SIDE, SIDE, HEIGHT), ((0, 16),), -0.2, 0.2), 0.0, 1.0)
    velocity = draw_velocity(jax.random.fold_in(jax.random.fold_in(streams_of[8], part), 71), part)
    interface_flags = touch_ends((jax.random.randint(part_keys[3], (BLOCKS, SIDE, SIDE, HEIGHT), 0, 4) < 1).astype(jnp.int32), jax.random.fold_in(part_keys[3], 1), 0, 1)
    block_links = draw_block_links(jax.random.fold_in(streams_of[8], 71), part)
    deck_node = touch_ends(jax.random.randint(streams_of[5], (BLOCKS, SIDE, SIDE), 0, NODES), jax.random.fold_in(streams_of[5], 1), 0, NODES - 1).astype(jnp.int32)
    mode_shapes = centred(streams_of[6], (MODES, NODES), 1.0, 4.0, jnp.float32)
    mobility = jnp.clip(jnp.exp(jax.random.uniform(streams_of[7], (MODES,), jnp.float32, math.log(0.3), math.log(3.0))), 0.3, 3.0)
    return {"fraction": fraction, "fraction_start": fraction_start, "velocity": velocity, "interface_flags": interface_flags, "block_links": block_links, "deck_node": deck_node, "mode_shapes": mode_shapes, "mobility": mobility}


CFL_NUMBER = 0.4
SHARPEN = 2.0
DECK_GAIN = 0.15
EPSILON = 1e-06

def minmod(first, second):
    return 0.5 * (jnp.sign(first) + jnp.sign(second)) * jnp.minimum(jnp.abs(first), jnp.abs(second))

def upwind(far_left, left_cell, right_cell, far_right, face_speed):
    left_value = left_cell + 0.5 * minmod(left_cell - far_left, right_cell - left_cell)
    right_value = right_cell - 0.5 * minmod(right_cell - left_cell, far_right - right_cell)
    return jnp.maximum(face_speed, 0.0) * left_value + jnp.minimum(face_speed, 0.0) * right_value

def face_layers(fill, flow_field):
    first = jnp.stack([fill[:, 0], fill[:, 1], -flow_field[:, 0, 0]], 1)
    second = jnp.stack([fill[:, -1], fill[:, -2], flow_field[:, 0, -1]], 1)
    third = jnp.stack([fill[:, :, 0], fill[:, :, 1], -flow_field[:, 1, :, 0]], 1)
    fourth = jnp.stack([fill[:, :, -1], fill[:, :, -2], flow_field[:, 1, :, -1]], 1)
    return jnp.stack([first, second, third, fourth], 1)

def block_rate(fill, flow_field, ghosts, deck_value):
    padded = jnp.concatenate([ghosts[0, 1][None], ghosts[0, 0][None], fill, ghosts[1, 0][None], ghosts[1, 1][None]], 0)
    speeds = jnp.concatenate([ghosts[0, 2][None], flow_field[0], -ghosts[1, 2][None]], 0)
    flux_i = upwind(padded[:-3], padded[1:-2], padded[2:-1], padded[3:], 0.5 * (speeds[:-1] + speeds[1:]))
    padded_j = jnp.concatenate([ghosts[2, 1][:, None], ghosts[2, 0][:, None], fill, ghosts[3, 0][:, None], ghosts[3, 1][:, None]], 1)
    speeds_j = jnp.concatenate([ghosts[2, 2][:, None], flow_field[1], -ghosts[3, 2][:, None]], 1)
    flux_j = upwind(padded_j[:, :-3], padded_j[:, 1:-2], padded_j[:, 2:-1], padded_j[:, 3:], 0.5 * (speeds_j[:, :-1] + speeds_j[:, 1:]))
    edged = jnp.concatenate([fill[:, :, :1], fill, fill[:, :, -1:]], 2)
    vertical = flow_field[2]
    inner = upwind(edged[:, :, :-3], edged[:, :, 1:-2], edged[:, :, 2:-1], edged[:, :, 3:], 0.5 * (vertical[:, :, :-1] + vertical[:, :, 1:]))
    bottom = jnp.zeros_like(fill[:, :, :1])
    top = deck_value[:, :, None] * fill[:, :, -1:]
    flux_k = jnp.concatenate([bottom, inner, top], 2)
    return -(flux_i[1:] - flux_i[:-1] + (flux_j[:, 1:] - flux_j[:, :-1]) + (flux_k[:, :, 1:] - flux_k[:, :, :-1]))

def reference(fraction, fraction_start, velocity, interface_flags, block_links, deck_node, mode_shapes, mobility):
    flow_field = velocity.astype(jnp.float32)
    layers = face_layers(fraction, flow_field)
    ghosts = layers[block_links[:, :, 0], block_links[:, :, 1]]
    ghosts = jnp.where(block_links[:, :, 2][:, :, None, None, None] == 1, ghosts[:, :, :, ::-1, :], ghosts)
    top_fill = fraction[:, :, :, -1]
    top_vertical = flow_field[:, 2, :, :, -1]
    pressure = top_fill * (1.0 + top_vertical * top_vertical)
    nodal = jax.ops.segment_sum(pressure.reshape(-1), deck_node.reshape(-1), num_segments=NODES)
    scale = math.sqrt(NODES) / (BLOCKS * SIDE * SIDE)
    modal_force = jnp.dot(mode_shapes, nodal, precision=lax.Precision.HIGHEST) * scale
    modal_speed = mobility * modal_force
    node_speed = jnp.dot(modal_speed, mode_shapes, precision=lax.Precision.HIGHEST)
    deck_speed = jnp.tanh(DECK_GAIN * node_speed[deck_node])
    rates = lax.map(lambda items: block_rate(*items), (fraction, flow_field, ghosts, deck_speed))
    fill = fraction
    rates = rates + SHARPEN * interface_flags.astype(jnp.float32) * fill * (1.0 - fill) * (2.0 * fill - 1.0)
    time_step = CFL_NUMBER / (jnp.max(jnp.abs(flow_field)) + EPSILON)
    updated = 0.75 * fraction_start + 0.25 * (fraction + time_step * rates)
    return (updated, deck_speed)
```

```python
import functools
import math

import jax
import jax.numpy as jnp
from jax import lax
from jax.experimental import pallas as pl
from jax.experimental.pallas import tpu as pltpu
from jax.sharding import PartitionSpec as P

CAP = 4
CFL_NUMBER = 0.4
SHARPEN = 2.0
DECK_GAIN = 0.15
EPSILON = 1e-06
LANES = 128
VMEM_LIMIT = 40 * 1024 * 1024


def swapped(x, axis, stride):
    return lax.ppermute(x, axis, [(i, i ^ 1 << stride) for i in range(lax.axis_size(axis))])


def limited(first, second):
    return jnp.maximum(jnp.minimum(second, jnp.maximum(first, 0.0)), jnp.minimum(first, 0.0))


def set_bits(x):
    x = x - ((x >> 1) & 0x5555)
    x = (x & 0x3333) + ((x >> 2) & 0x3333)
    x = (x + (x >> 4)) & 0x0F0F
    return (x + (x >> 8)) & 0x1F


def route(links, me, blocks, bits, count, mask, sent, got):
    for k in range(bits):
        count[k] = 0
        mask[k] = 0
        for s in range(CAP):
            sent[k * CAP + s] = 0
            got[k * CAP + s] = -1
    shift = blocks.bit_length() - 1
    found = []
    for face in range(4 * blocks):
        b, t = face // 4, face % 4
        partner = links[b, t, 0]
        differ = (partner >> shift) ^ me
        k = jnp.int32(0)
        for q in range(1, bits):
            k = k + (differ >= (1 << q)).astype(jnp.int32)
        r = count[k]
        count[k] = r + 1
        sent[k * CAP + r] = face
        source = (partner & (blocks - 1)) * 4 + links[b, t, 1]
        mask[k] = mask[k] | (jnp.int32(1) << source)
        found.append((k, source))
    for face, (k, source) in enumerate(found):
        rank = set_bits(mask[k] & ((jnp.int32(1) << source) - 1))
        got[k * CAP + rank] = 2 * face + links[face // 4, face % 4, 2]


def pack_kernel(dims, links, node_ref, shapes_ref, fill_hbm, vel_hbm, *rest):
    blocks, ext, height, bits = dims
    outs = rest[:bits]
    red_ref, got, fill, vel, edge, left, right, count, mask, sent, sems = rest[bits:]
    area = ext * ext
    fill_copies, vel_copies = [], []
    for b in range(blocks):
        fill_copies.append(pltpu.make_async_copy(fill_hbm.at[b], fill.at[b], sems.at[0, b]))
        vel_copies.append(pltpu.make_async_copy(vel_hbm.at[b], vel.at[b], sems.at[1, b]))
        fill_copies[b].start()
        vel_copies[b].start()
    route(links, lax.axis_index("family"), blocks, bits, count, mask, sent, got)
    lane = lax.broadcasted_iota(jnp.int32, (ext, height), 1)
    rows = fill.reshape(blocks * area, height)
    pressure = jnp.zeros((ext, height), jnp.float32)
    speed = jnp.zeros((ext, height), jnp.bfloat16)
    for b in range(blocks):
        fill_copies[b].wait()
        vel_copies[b].wait()
        for side in range(2):
            x = vel[b, 1, :, side * (ext - 8) : side * (ext - 8) + 8, :].astype(jnp.float32)
            edge[pl.ds((b * 2 + side) * ext * 8, ext * 8), :] = x.reshape(ext * 8, height)

        def step(i, carry):
            pressure, speed = carry
            up = vel[b, 2, i]
            speed = jnp.maximum(speed, jnp.abs(vel[b, 0, i]))
            speed = jnp.maximum(speed, jnp.abs(vel[b, 1, i]))
            speed = jnp.maximum(speed, jnp.abs(up))
            up = up.astype(jnp.float32)
            push = fill[b, i] * (1.0 + up * up)
            at = b * ext + i
            pressure = jnp.where(lane == at, pltpu.roll(push, at + 1, 1), pressure)
            return pressure, speed

        pressure, speed = lax.fori_loop(0, ext, step, (pressure, speed), unroll=4)
    for k in range(bits):
        for s in range(CAP):
            face = sent[k * CAP + s]
            b, t = face >> 2, face & 3
            side = t & 1
            sign = (2 * side - 1).astype(jnp.float32)
            near = side * (ext - 1)
            after = near + 1 - 2 * side

            @pl.when(t < 2)
            def _():
                outs[k][s, 0] = fill[b, near]
                outs[k][s, 1] = fill[b, after]
                outs[k][s, 2] = vel[b, 0, near].astype(jnp.float32) * sign

            @pl.when(t >= 2)
            def _():
                outs[k][s, 0] = rows[pl.ds(b * area + near, ext, stride=ext), :]
                outs[k][s, 1] = rows[pl.ds(b * area + after, ext, stride=ext), :]
                outs[k][s, 2] = edge[pl.ds((b * 2 + side) * ext * 8 + side * 7, ext, stride=8), :] * sign

    node = node_ref[...].T
    high, low = node >> 7, node & 127
    groups = shapes_ref.shape[1] // LANES
    part = pressure.astype(jnp.bfloat16)
    first = part.astype(jnp.float32)
    second = pressure - first
    high_at = lax.broadcasted_iota(jnp.int32, (groups, height), 0)
    low_at = lax.broadcasted_iota(jnp.int32, (LANES, height), 0)
    for j in range(ext):
        cols = pl.ds(j * height, height)
        same = high_at == high[j : j + 1]
        left[0:groups, cols] = jnp.where(same, first[j : j + 1], 0.0).astype(jnp.bfloat16)
        left[groups : 2 * groups, cols] = jnp.where(same, second[j : j + 1], 0.0).astype(jnp.bfloat16)
        right[:, cols] = jnp.where(low_at == low[j : j + 1], 1.0, 0.0).astype(jnp.bfloat16)
    nodal = lax.dot_general(left[...], right[...], (((1,), (1,)), ((), ())), preferred_element_type=jnp.float32)
    nodal = nodal[:groups] + nodal[groups:]
    lane8 = lax.broadcasted_iota(jnp.int32, (8, LANES), 1)
    tiles = shapes_ref.shape[0] // 8
    top = jnp.max(jnp.max(speed.astype(jnp.float32), axis=0, keepdims=True), axis=1, keepdims=True)
    red = jnp.where(lane8 == tiles, top, 0.0)
    for t in range(tiles):
        total = jnp.zeros((8, LANES), jnp.float32)
        for g in range(groups):
            total = total + shapes_ref[8 * t : 8 * t + 8, g * LANES : (g + 1) * LANES] * nodal[g : g + 1]
        red = jnp.where(lane8 == t, jnp.sum(total, axis=1, keepdims=True), red)
    red_ref[...] = red


def rates_kernel(dims, fill_hbm, start_hbm, vel_hbm, flag_hbm, base_ref, rate_ref, rim_ref, fill, start, vel, flag, edge, sems):
    blocks, ext, height, bits = dims
    area = ext * ext
    copies = []
    for b in range(blocks):
        group = [
            pltpu.make_async_copy(fill_hbm.at[b], fill.at[b], sems.at[0, b]),
            pltpu.make_async_copy(vel_hbm.at[b], vel.at[b], sems.at[1, b]),
            pltpu.make_async_copy(flag_hbm.at[b], flag.at[b], sems.at[2, b]),
            pltpu.make_async_copy(start_hbm.at[b], start.at[b], sems.at[3, b]),
        ]
        for c in group:
            c.start()
        copies.append(group)
    lane = lax.broadcasted_iota(jnp.int32, (ext, height), 1)
    row = lax.broadcasted_iota(jnp.int32, (ext, height), 0)
    last_lane = lane == height - 1
    open_row = (row >= 1) & (row <= ext - 3)
    rows = fill.reshape(blocks * area, height)

    def across(f, h, u, axis, size, cut, masked):
        step = jnp.where(cut, 0.0, pltpu.roll(h, size - 1, axis) - h) if masked else pltpu.roll(h, size - 1, axis) - h
        slope = limited(pltpu.roll(step, 1, axis), step)
        behind = f - slope
        v = u + pltpu.roll(u, size - 1, axis)
        v = jnp.where(cut, 0.0, v)
        flux = v * jnp.where(v > 0.0, f + slope, pltpu.roll(behind, size - 1, axis))
        return pltpu.roll(flux, 1, axis) - flux

    def own(b, i, f, h):
        rate = across(f, h, vel[b, 2, i].astype(jnp.float32), 1, height, last_lane, True)
        rate = rate + across(f, h, vel[b, 1, i].astype(jnp.float32), 0, ext, ~open_row, False)
        sharp = (2.0 * SHARPEN) * f * (1.0 - f) * (2.0 * f - 1.0)
        rate = rate + jnp.where(flag[b, i] != 0, sharp, 0.0)
        base_ref[b, i] = 0.75 * start[b, i] + 0.25 * f
        return rate

    for b in range(blocks):
        for c in copies[b]:
            c.wait()
        f0 = fill[b, 0]
        rate_ref[b, 0] = own(b, 0, f0, 0.5 * f0)
        f1 = fill[b, 1]
        h1 = 0.5 * f1
        rate1 = own(b, 1, f1, h1)
        f2 = fill[b, 2]
        h2 = 0.5 * f2
        step = h2 - h1
        ahead = f1 + limited(h1 - 0.5 * f0, step)

        def layer(i, carry):
            f, h, step_before, ahead, flux_before, u_before, rate_before = carry
            f_next = fill[b, i + 1]
            h_next = 0.5 * f_next
            step = h_next - h
            slope = limited(step_before, step)
            u = vel[b, 0, i].astype(jnp.float32)
            v = u_before + u
            flux = v * jnp.where(v > 0.0, ahead, f - slope)
            rate_ref[b, i - 1] = rate_before + (flux_before - flux)
            return f_next, h_next, step, f + slope, flux, u, own(b, i, f, h)

        carry = (f2, h2, step, ahead, jnp.zeros_like(f0), vel[b, 0, 1].astype(jnp.float32), rate1)
        carry = lax.fori_loop(2, ext - 1, layer, carry)
        f, h, _, _, flux, _, rate = carry
        rate_ref[b, ext - 2] = rate + flux
        rate_ref[b, ext - 1] = own(b, ext - 1, f, h)

        for side in range(2):
            x = vel[b, 1, :, side * (ext - 8) : side * (ext - 8) + 8, :].astype(jnp.float32)
            edge[pl.ds(side * ext * 8, ext * 8), :] = x.reshape(ext * 8, height)
        for t in range(4):
            side = t % 2
            sign = 1.0 - 2.0 * side
            at = [side * (ext - 1) + d * (1 - 2 * side) for d in range(3)]
            if t < 2:
                cells = [fill[b, i] for i in at]
                flows = [vel[b, 0, i].astype(jnp.float32) * sign for i in at[:2]]
            else:
                cells = [rows[pl.ds(b * area + j, ext, stride=ext), :] for j in at]
                flows = [edge[pl.ds(side * ext * 8 + j % 8, ext, stride=8), :] * sign for j in at[:2]]
            step = 0.5 * (cells[1] - cells[0])
            slope = limited(step, 0.5 * (cells[2] - cells[1]))
            rim_ref[4 * b + t, 0] = cells[0]
            rim_ref[4 * b + t, 1] = step
            rim_ref[4 * b + t, 2] = cells[1] - slope
            rim_ref[4 * b + t, 3] = flows[0]
            rim_ref[4 * b + t, 4] = flows[0] + flows[1]


def final_kernel(dims, devices, got, mobility_ref, node_ref, shapes_ref, red_ref, base_ref, rate_ref, rim_ref, fill_hbm, *rest):
    blocks, ext, height, bits = dims
    ghosts = rest[:bits]
    out_hbm, deck_ref, ghost, out, top_fill, sems, fsems = rest[bits:]
    area = ext * ext
    tiles = shapes_ref.shape[0] // 8
    groups = shapes_ref.shape[1] // LANES
    fill_copies = [pltpu.make_async_copy(fill_hbm.at[b], top_fill.at[b], fsems.at[b]) for b in range(blocks)]
    for c in fill_copies:
        c.start()
    turned = 7 - lax.broadcasted_iota(jnp.int32, (8, height), 0)
    for k in range(bits):
        for s in range(CAP):
            code = got[k * CAP + s]
            face, flip = code >> 1, code & 1

            @pl.when((code >= 0) & (flip == 0))
            def _():
                ghost[face] = ghosts[k][s]

            @pl.when((code >= 0) & (flip == 1))
            def _():
                for c in range(3):
                    for q in range(ext // 8):
                        x = ghosts[k][s, c, ext - 8 - 8 * q : ext - 8 * q, :]
                        ghost[face, c, 8 * q : 8 * q + 8, :] = jnp.take_along_axis(x, turned, axis=0)

    red = red_ref[...]
    time_step = CFL_NUMBER / (red[0:1, tiles : tiles + 1] + EPSILON)
    eighth = 0.125 * time_step
    scale = math.sqrt(shapes_ref.shape[1]) / (blocks * devices * area)
    lane8 = lax.broadcasted_iota(jnp.int32, (8, LANES), 1)
    sub8 = lax.broadcasted_iota(jnp.int32, (8, LANES), 0)
    mobility = mobility_ref[...]
    sums = [jnp.zeros((8, LANES), jnp.float32) for _ in range(groups)]
    width = mobility.shape[1]
    for t in range(tiles):
        pick = lax.broadcasted_iota(jnp.int32, (8, width), 1) == 8 * t + lax.broadcasted_iota(jnp.int32, (8, width), 0)
        gain = jnp.sum(jnp.where(pick, mobility, 0.0), axis=1, keepdims=True)
        speed = jnp.broadcast_to(gain * (red[:, t : t + 1] * scale), (8, LANES))
        for g in range(groups):
            sums[g] = sums[g] + shapes_ref[8 * t : 8 * t + 8, g * LANES : (g + 1) * LANES] * speed
    node = node_ref[...].T
    high, low = node >> 7, node & 127
    deck = jnp.zeros((ext, height), jnp.float32)
    for g in range(groups):
        line = jnp.broadcast_to(jnp.sum(sums[g], axis=0, keepdims=True), (8, LANES))
        values = [jnp.take_along_axis(line, low[8 * q : 8 * q + 8], axis=1) for q in range(ext // 8)]
        deck = jnp.where(high == g, jnp.concatenate(values, 0), deck)
    deck = jnp.tanh(DECK_GAIN * deck)
    deck_ref[...] = deck.T
    lane = lax.broadcasted_iota(jnp.int32, (ext, height), 1)
    last_lane = lane == height - 1
    rows = out.reshape(blocks * area, height)
    twice = 2.0 * eighth
    deck = deck * twice

    def apply(ghost_face, rim_face):
        g0, g1, gv = ghost[ghost_face, 0], ghost[ghost_face, 1], ghost[ghost_face, 2]
        c0, step1, behind1, u0, v1 = (rim_ref[rim_face, q] for q in range(5))
        step0 = 0.5 * (c0 - g0)
        ghost_slope = limited(step0, 0.5 * (g0 - g1))
        slope = limited(step0, step1)
        v0 = gv + u0
        flux0 = v0 * jnp.where(v0 > 0.0, g0 + ghost_slope, c0 - slope)
        flux1 = v1 * jnp.where(v1 > 0.0, c0 + slope, behind1)
        return eighth * (flux0 - flux1), eighth * flux1

    copies = []
    for b in range(blocks):
        fill_copies[b].wait()

        def layer(i, carry):
            at = b * ext + i
            lid = jnp.where(last_lane, pltpu.roll(deck, height - 1 - at, 1), 0.0)
            out[b, i] = base_ref[b, i] + eighth * rate_ref[b, i] - lid * top_fill[b, i]
            return carry

        lax.fori_loop(0, ext, layer, 0, unroll=4)
        for t in range(4):
            side = t % 2
            near = side * (ext - 1)
            after = near + 1 - 2 * side
            add0, add1 = apply(4 * b + t, 4 * b + t)
            for where, add in ((near, add0), (after, add1)):
                if t < 2:
                    out[b, where] = out[b, where] + add
                else:
                    line = pl.ds(b * area + where, ext, stride=ext)
                    rows[line, :] = rows[line, :] + add
        copy = pltpu.make_async_copy(out.at[b], out_hbm.at[b], sems.at[b])
        copy.start()
        copies.append(copy)
    for copy in copies:
        copy.wait()


def local(fraction, fraction_start, velocity, interface_flags, block_links, deck_node, mode_shapes, mobility):
    blocks, ext, _, height = fraction.shape
    devices = lax.axis_size("family")
    bits = devices.bit_length() - 1
    modes, nodes = mode_shapes.shape
    faces = 4 * blocks
    dims = (blocks, ext, height, bits)
    f32 = jnp.float32
    vmem = pl.BlockSpec(memory_space=pltpu.VMEM)
    smem = pl.BlockSpec(memory_space=pltpu.SMEM)
    hbm = pl.BlockSpec(memory_space=pl.ANY)
    params = pltpu.CompilerParams(vmem_limit_bytes=VMEM_LIMIT)
    flat_node = deck_node.reshape(blocks * ext, ext)
    packed = pl.pallas_call(
        functools.partial(pack_kernel, dims),
        out_shape=[jax.ShapeDtypeStruct((CAP, 3, ext, height), f32)] * bits
        + [jax.ShapeDtypeStruct((8, LANES), f32), jax.ShapeDtypeStruct((bits * CAP,), jnp.int32)],
        in_specs=[smem, vmem, vmem, hbm, hbm],
        out_specs=[vmem] * (bits + 1) + [smem],
        scratch_shapes=[
            pltpu.VMEM((blocks, ext, ext, height), f32),
            pltpu.VMEM((blocks, 3, ext, ext, height), jnp.bfloat16),
            pltpu.VMEM((blocks * 2 * ext * 8, height), f32),
            pltpu.VMEM((2 * nodes // LANES, ext * height), jnp.bfloat16),
            pltpu.VMEM((LANES, ext * height), jnp.bfloat16),
            pltpu.SMEM((bits,), jnp.int32),
            pltpu.SMEM((bits,), jnp.int32),
            pltpu.SMEM((bits * CAP,), jnp.int32),
            pltpu.SemaphoreType.DMA((2, blocks)),
        ],
        compiler_params=params,
        name="pack",
    )(block_links, flat_node, mode_shapes, fraction, velocity)
    outgoing, red, got = packed[:bits], packed[bits], packed[bits + 1]
    received = [None] * bits
    for k in reversed(range(bits)):
        received[k] = swapped(outgoing[k], "family", k)
    is_top = lax.broadcasted_iota(jnp.int32, red.shape, 1) == modes // 8
    for k in range(bits):
        other = swapped(red, "family", k)
        red = jnp.where(is_top, jnp.maximum(red, other), red + other)
    base, rate, rim = pl.pallas_call(
        functools.partial(rates_kernel, dims),
        out_shape=[
            jax.ShapeDtypeStruct(fraction.shape, f32),
            jax.ShapeDtypeStruct(fraction.shape, f32),
            jax.ShapeDtypeStruct((faces, 5, ext, height), f32),
        ],
        in_specs=[hbm] * 4,
        out_specs=[vmem] * 3,
        scratch_shapes=[
            pltpu.VMEM((blocks, ext, ext, height), f32),
            pltpu.VMEM((blocks, ext, ext, height), f32),
            pltpu.VMEM((blocks, 3, ext, ext, height), jnp.bfloat16),
            pltpu.VMEM((blocks, ext, ext, height), jnp.int32),
            pltpu.VMEM((2 * ext * 8, height), f32),
            pltpu.SemaphoreType.DMA((4, blocks)),
        ],
        compiler_params=params,
        cost_estimate=pl.CostEstimate(flops=80 * fraction.size, bytes_accessed=20 * fraction.size, transcendentals=0),
        name="rates",
    )(fraction, fraction_start, velocity, interface_flags)
    updated, deck = pl.pallas_call(
        functools.partial(final_kernel, dims, devices),
        out_shape=[
            jax.ShapeDtypeStruct(fraction.shape, f32),
            jax.ShapeDtypeStruct((blocks * ext, ext), f32),
        ],
        in_specs=[smem] + [vmem] * 7 + [hbm] + [vmem] * bits,
        out_specs=[hbm, vmem],
        scratch_shapes=[
            pltpu.VMEM((faces, 3, ext, height), f32),
            pltpu.VMEM((blocks, ext, ext, height), f32),
            pltpu.VMEM((blocks, ext, ext, height), f32),
            pltpu.SemaphoreType.DMA((blocks,)),
            pltpu.SemaphoreType.DMA((blocks,)),
        ],
        compiler_params=params,
        name="finish",
    )(got, mobility.reshape(1, modes), flat_node, mode_shapes, red, base, rate, rim, fraction, *received)
    return updated, deck.reshape(blocks, ext, ext)


def solution(mesh):
    in_specs = (
        P(("groups", "family"), None, None, None),
        P(("groups", "family"), None, None, None),
        P(("groups", "family"), None, None, None, None),
        P(("groups", "family"), None, None, None),
        P("family", None, None),
        P("family", None, None),
        P(),
        P(),
    )
    out_specs = (P(("groups", "family"), None, None, None), P(("groups", "family"), None, None))
    return jax.shard_map(local, mesh=mesh, in_specs=in_specs, out_specs=out_specs, check_vma=False)
```

```python
import functools
import math

import jax
import jax.numpy as jnp
import numpy as np
from jax import lax
from jax.experimental import pallas as pl
from jax.experimental.pallas import tpu as pltpu
from jax.sharding import PartitionSpec as P

CAP = 4
CFL_NUMBER = 0.4
SHARPEN = 2.0
DECK_GAIN = 0.15
EPSILON = 1e-06
LANES = 128
MIB = 1024 * 1024


def swapped(x, axis, stride):
    return lax.ppermute(x, axis, [(i, i ^ 1 << stride) for i in range(lax.axis_size(axis))])


def limited(first, second):
    return jnp.maximum(jnp.minimum(second, jnp.maximum(first, 0.0)), jnp.minimum(first, 0.0))


def set_bits(x):
    x = x - ((x >> 1) & 0x5555)
    x = (x & 0x3333) + ((x >> 2) & 0x3333)
    x = (x + (x >> 4)) & 0x0F0F
    return (x + (x >> 8)) & 0x1F


def route(links, me, blocks, bits, count, mask, sent, got):
    for k in range(bits):
        count[k] = 0
        mask[k] = 0
        for s in range(CAP):
            sent[k * CAP + s] = 0
            got[k * CAP + s] = -1
    shift = blocks.bit_length() - 1
    found = []
    for face in range(4 * blocks):
        b, t = face // 4, face % 4
        partner = links[0, b, t]
        differ = (partner >> shift) ^ me
        k = jnp.int32(0)
        for q in range(1, bits):
            k = k + (differ >= (1 << q)).astype(jnp.int32)
        r = count[k]
        count[k] = r + 1
        sent[k * CAP + r] = face
        source = (partner & (blocks - 1)) * 4 + links[1, b, t]
        mask[k] = mask[k] | (jnp.int32(1) << source)
        found.append((k, source))
    for face, (k, source) in enumerate(found):
        rank = set_bits(mask[k] & ((jnp.int32(1) << source) - 1))
        got[k * CAP + rank] = 2 * face + links[2, face // 4, face % 4]


def pack_kernel(dims, links, node_hbm, shapes_hbm, fill_hbm, vel_hbm, *rest):
    blocks, ext, height, bits = dims
    outs = rest[:bits]
    red_ref, got, fill, vel, edge, left, right, node_ref, shapes_ref, count, mask, sent, sems, late = rest[bits:]
    area = ext * ext
    fill_copies, vel_copies = [], []
    for b in range(blocks):
        fill_copies.append(pltpu.make_async_copy(fill_hbm.at[b], fill.at[b], sems.at[0, b]))
        vel_copies.append(pltpu.make_async_copy(vel_hbm.at[b], vel.at[b], sems.at[1, b]))
        vel_copies[b].start()
        fill_copies[b].start()
    late_copies = [
        pltpu.make_async_copy(node_hbm, node_ref, late.at[0]),
        pltpu.make_async_copy(shapes_hbm, shapes_ref, late.at[1]),
    ]
    for c in late_copies:
        c.start()
    route(links, lax.axis_index("family"), blocks, bits, count, mask, sent, got)
    lane = lax.broadcasted_iota(jnp.int32, (ext, height), 1)
    rows = fill.reshape(blocks * area, height)
    pressure = jnp.zeros((ext, height), jnp.float32)
    speed = jnp.zeros((ext, height), jnp.bfloat16)
    for b in range(blocks):
        fill_copies[b].wait()
        vel_copies[b].wait()
        for side in range(2):
            x = vel[b, 1, :, side * (ext - 8) : side * (ext - 8) + 8, :].astype(jnp.float32)
            edge[pl.ds((b * 2 + side) * ext * 8, ext * 8), :] = x.reshape(ext * 8, height)

        def step(i, carry):
            pressure, speed = carry
            up = vel[b, 2, i]
            speed = jnp.maximum(speed, jnp.abs(vel[b, 0, i]))
            speed = jnp.maximum(speed, jnp.abs(vel[b, 1, i]))
            speed = jnp.maximum(speed, jnp.abs(up))
            up = up.astype(jnp.float32)
            push = fill[b, i] * (1.0 + up * up)
            at = b * ext + i
            pressure = jnp.where(lane == at, pltpu.roll(push, at + 1, 1), pressure)
            return pressure, speed

        pressure, speed = lax.fori_loop(0, ext, step, (pressure, speed), unroll=True)
    for k in range(bits):
        for s in range(CAP):
            face = sent[k * CAP + s]
            b, t = face >> 2, face & 3
            side = t & 1
            sign = (2 * side - 1).astype(jnp.float32)
            near = side * (ext - 1)
            after = near + 1 - 2 * side

            @pl.when(t < 2)
            def _():
                outs[k][s, 0] = fill[b, near]
                outs[k][s, 1] = fill[b, after]
                outs[k][s, 2] = vel[b, 0, near].astype(jnp.float32) * sign

            @pl.when(t >= 2)
            def _():
                outs[k][s, 0] = rows[pl.ds(b * area + near, ext, stride=ext), :]
                outs[k][s, 1] = rows[pl.ds(b * area + after, ext, stride=ext), :]
                outs[k][s, 2] = edge[pl.ds((b * 2 + side) * ext * 8 + side * 7, ext, stride=8), :] * sign

    for c in late_copies:
        c.wait()
    node = node_ref[...].T
    high, low = node >> 7, node & 127
    groups = shapes_ref.shape[1] // LANES
    part = pressure.astype(jnp.bfloat16)
    first = part.astype(jnp.float32)
    second = pressure - first
    high_at = lax.broadcasted_iota(jnp.int32, (groups, height), 0)
    low_at = lax.broadcasted_iota(jnp.int32, (LANES, height), 0)
    for j in range(ext):
        cols = pl.ds(j * height, height)
        same = high_at == high[j : j + 1]
        left[0:groups, cols] = jnp.where(same, first[j : j + 1], 0.0).astype(jnp.bfloat16)
        left[groups : 2 * groups, cols] = jnp.where(same, second[j : j + 1], 0.0).astype(jnp.bfloat16)
        right[:, cols] = jnp.where(low_at == low[j : j + 1], 1.0, 0.0).astype(jnp.bfloat16)
    nodal = lax.dot_general(left[...], right[...], (((1,), (1,)), ((), ())), preferred_element_type=jnp.float32)
    nodal = nodal[:groups] + nodal[groups:]
    lane8 = lax.broadcasted_iota(jnp.int32, (8, LANES), 1)
    tiles = shapes_ref.shape[0] // 8
    top = jnp.max(jnp.max(speed.astype(jnp.float32), axis=0, keepdims=True), axis=1, keepdims=True)
    red = jnp.where(lane8 == tiles, top, 0.0)
    for t in range(tiles):
        total = jnp.zeros((8, LANES), jnp.float32)
        for g in range(groups):
            total = total + shapes_ref[8 * t : 8 * t + 8, g * LANES : (g + 1) * LANES] * nodal[g : g + 1]
        red = jnp.where(lane8 == t, jnp.sum(total, axis=1, keepdims=True), red)
    red_ref[...] = red


def shift_tables(height):
    k = np.arange(height)
    eye = np.eye(height, dtype=np.float32)
    nxt = np.eye(height, k=-1, dtype=np.float32)
    nxt2 = np.eye(height, k=-2, dtype=np.float32)
    prv = np.eye(height, k=1, dtype=np.float32)
    before = 0.5 * (eye - prv); before[:, 0] = 0
    step = 0.5 * (nxt - eye); step[:, -1] = 0
    after = 0.5 * (nxt2 - nxt); after[:, -2:] = 0
    cells = np.concatenate([before, step, after, nxt], 1)
    flow = nxt + eye; flow[:, -1] = 0
    return np.concatenate([cells, cells], 0), flow
def rates_kernel(dims, cells_ref, flow_ref, fill, vel, start, flag, base_ref, rate_ref, rim_ref, top_ref, edge, lift):
    blocks, ext, height, bits = dims
    area = ext * ext
    lane = lax.broadcasted_iota(jnp.int32, (ext, height), 1)
    row = lax.broadcasted_iota(jnp.int32, (ext, height), 0)
    open_row = (row >= 1) & (row <= ext - 3)
    rows = fill.reshape(blocks * area, height)
    layers = 8
    size = layers * ext
    top = jnp.zeros((ext, height), jnp.float32)
    def block(b, top):

        def column(c, carry):
            x = fill[b, pl.ds(c * layers, layers)].reshape(size, height)
            u = vel[b, 2, pl.ds(c * layers, layers)].reshape(size, height)
            high = x.astype(jnp.bfloat16)
            low = (x - high.astype(jnp.float32)).astype(jnp.bfloat16)
            y = jnp.dot(jnp.concatenate([high, low], 1), cells_ref[...], preferred_element_type=jnp.float32)
            v = jnp.dot(u, flow_ref[...], preferred_element_type=jnp.float32)
            step = y[:, height : 2 * height]
            ahead = x + limited(step, y[:, :height])
            behind = y[:, 3 * height :] - limited(step, y[:, 2 * height : 3 * height])
            lift[pl.ds(c * layers, layers)] = (v * jnp.where(v > 0.0, ahead, behind)).reshape(layers, ext, height)
            return carry

        lax.fori_loop(0, ext // layers, column, 0, unroll=True)

        def own(i, f, h):
            flux = lift[i]
            rate = pltpu.roll(flux, 1, 1) - flux
            step = pltpu.roll(h, ext - 1, 0) - h
            slope = limited(pltpu.roll(step, 1, 0), step)
            u = vel[b, 1, i].astype(jnp.float32)
            v = u + pltpu.roll(u, ext - 1, 0)
            v = jnp.where(open_row, v, 0.0)
            flux = v * jnp.where(v > 0.0, f + slope, pltpu.roll(f - slope, ext - 1, 0))
            rate = rate + (pltpu.roll(flux, 1, 0) - flux)
            sharp = (f * (1.0 - f)) * ((4.0 * SHARPEN) * f - 2.0 * SHARPEN)
            rate = rate + jnp.where(flag[b, i] != 0, sharp, 0.0)
            base_ref[b, i] = 0.75 * start[b, i] + 0.25 * f
            return rate

        def picked(i, f, top):
            at = b * ext + i
            return jnp.where(lane == at, pltpu.roll(f, at + 1, 1), top)

        f0 = fill[b, 0]
        rate_ref[b, 0] = own(0, f0, 0.5 * f0)
        top = picked(0, f0, top)
        f1 = fill[b, 1]
        h1 = 0.5 * f1
        rate1 = own(1, f1, h1)
        top = picked(1, f1, top)
        f2 = fill[b, 2]
        h2 = 0.5 * f2
        step = h2 - h1
        ahead = f1 + limited(h1 - 0.5 * f0, step)

        def layer(i, carry):
            f, h, step_before, ahead, flux_before, u_before, rate_before, top = carry
            f_next = fill[b, i + 1]
            h_next = 0.5 * f_next
            step = h_next - h
            slope = limited(step_before, step)
            u = vel[b, 0, i].astype(jnp.float32)
            v = u_before + u
            flux = v * jnp.where(v > 0.0, ahead, f - slope)
            rate_ref[b, i - 1] = rate_before + (flux_before - flux)
            return f_next, h_next, step, f + slope, flux, u, own(i, f, h), picked(i, f, top)

        carry = (f2, h2, step, ahead, jnp.zeros_like(f0), vel[b, 0, 1].astype(jnp.float32), rate1, top)
        carry = lax.fori_loop(2, ext - 1, layer, carry, unroll=True)
        f, h, _, _, flux, _, rate, top = carry
        rate_ref[b, ext - 2] = rate + flux
        rate_ref[b, ext - 1] = own(ext - 1, f, h)
        top = picked(ext - 1, f, top)

        for side in range(2):
            x = vel[b, 1, :, side * (ext - 8) : side * (ext - 8) + 8, :].astype(jnp.float32)
            edge[pl.ds(side * ext * 8, ext * 8), :] = x.reshape(ext * 8, height)
        for t in range(4):
            side = t % 2
            sign = 1.0 - 2.0 * side
            at = [side * (ext - 1) + d * (1 - 2 * side) for d in range(3)]
            if t < 2:
                cells = [fill[b, i] for i in at]
                flows = [vel[b, 0, i].astype(jnp.float32) * sign for i in at[:2]]
            else:
                cells = [rows[pl.ds(b * area + j, ext, stride=ext), :] for j in at]
                flows = [edge[pl.ds(side * ext * 8 + j % 8, ext, stride=8), :] * sign for j in at[:2]]
            step = 0.5 * (cells[1] - cells[0])
            slope = limited(step, 0.5 * (cells[2] - cells[1]))
            rim_ref[4 * b + t, 0] = cells[0]
            rim_ref[4 * b + t, 1] = step
            rim_ref[4 * b + t, 2] = cells[1] - slope
            rim_ref[4 * b + t, 3] = flows[0]
            rim_ref[4 * b + t, 4] = flows[0] + flows[1]
        return top
    top_ref[...] = lax.fori_loop(0, blocks, block, top)


def final_kernel(dims, devices, got, mobility_ref, node_ref, shapes_ref, red_ref, base_ref, rate_ref, rim_ref, top_ref, *rest):
    blocks, ext, height, bits = dims
    ghosts = rest[:bits]
    out_hbm, deck_ref, ghost, out, sems = rest[bits:]
    area = ext * ext
    tiles = shapes_ref.shape[0] // 8
    groups = shapes_ref.shape[1] // LANES
    turned = 7 - lax.broadcasted_iota(jnp.int32, (8, height), 0)
    for k in range(bits):
        for s in range(CAP):
            code = got[k * CAP + s]
            face, flip = code >> 1, code & 1

            @pl.when((code >= 0) & (flip == 0))
            def _():
                ghost[face] = ghosts[k][s]

            @pl.when((code >= 0) & (flip == 1))
            def _():
                for c in range(3):
                    for q in range(ext // 8):
                        x = ghosts[k][s, c, ext - 8 - 8 * q : ext - 8 * q, :]
                        ghost[face, c, 8 * q : 8 * q + 8, :] = jnp.take_along_axis(x, turned, axis=0)

    red = red_ref[...]
    time_step = CFL_NUMBER / (red[0:1, tiles : tiles + 1] + EPSILON)
    eighth = 0.125 * time_step
    scale = math.sqrt(shapes_ref.shape[1]) / (blocks * devices * area)
    lane8 = lax.broadcasted_iota(jnp.int32, (8, LANES), 1)
    sub8 = lax.broadcasted_iota(jnp.int32, (8, LANES), 0)
    mobility = mobility_ref[...]
    sums = [jnp.zeros((8, LANES), jnp.float32) for _ in range(groups)]
    width = mobility.shape[1]
    for t in range(tiles):
        pick = lax.broadcasted_iota(jnp.int32, (8, width), 1) == 8 * t + lax.broadcasted_iota(jnp.int32, (8, width), 0)
        gain = jnp.sum(jnp.where(pick, mobility, 0.0), axis=1, keepdims=True)
        speed = jnp.broadcast_to(gain * (red[:, t : t + 1] * scale), (8, LANES))
        for g in range(groups):
            sums[g] = sums[g] + shapes_ref[8 * t : 8 * t + 8, g * LANES : (g + 1) * LANES] * speed
    node = node_ref[...].T
    high, low = node >> 7, node & 127
    deck = jnp.zeros((ext, height), jnp.float32)
    for g in range(groups):
        line = jnp.broadcast_to(jnp.sum(sums[g], axis=0, keepdims=True), (8, LANES))
        values = [jnp.take_along_axis(line, low[8 * q : 8 * q + 8], axis=1) for q in range(ext // 8)]
        deck = jnp.where(high == g, jnp.concatenate(values, 0), deck)
    deck = jnp.tanh(DECK_GAIN * deck)
    deck_ref[...] = deck.T
    lane = lax.broadcasted_iota(jnp.int32, (ext, height), 1)
    last_lane = lane == height - 1
    rows = out.reshape(blocks * area, height)
    deck = deck * (2.0 * eighth) * top_ref[...]

    def apply(ghost_face, rim_face):
        g0, g1, gv = ghost[ghost_face, 0], ghost[ghost_face, 1], ghost[ghost_face, 2]
        c0, step1, behind1, u0, v1 = (rim_ref[rim_face, q] for q in range(5))
        step0 = 0.5 * (c0 - g0)
        ghost_slope = limited(step0, 0.5 * (g0 - g1))
        slope = limited(step0, step1)
        v0 = gv + u0
        flux0 = v0 * jnp.where(v0 > 0.0, g0 + ghost_slope, c0 - slope)
        flux1 = v1 * jnp.where(v1 > 0.0, c0 + slope, behind1)
        return eighth * (flux0 - flux1), eighth * flux1

    copies = []
    for b in range(blocks):

        def layer(i, carry):
            at = b * ext + i
            lid = jnp.where(last_lane, pltpu.roll(deck, height - 1 - at, 1), 0.0)
            out[b, i] = base_ref[b, i] + eighth * rate_ref[b, i] - lid
            return carry

        lax.fori_loop(0, ext, layer, 0, unroll=True)
        for t in range(4):
            side = t % 2
            near = side * (ext - 1)
            after = near + 1 - 2 * side
            add0, add1 = apply(4 * b + t, 4 * b + t)
            for where, add in ((near, add0), (after, add1)):
                if t < 2:
                    out[b, where] = out[b, where] + add
                else:
                    line = pl.ds(b * area + where, ext, stride=ext)
                    rows[line, :] = rows[line, :] + add
        copy = pltpu.make_async_copy(out.at[b], out_hbm.at[b], sems.at[b])
        copy.start()
        copies.append(copy)
    for copy in copies:
        copy.wait()


def in_hbm(x):
    return pltpu.with_memory_space_constraint(x, pltpu.HBM)


def local(fraction, fraction_start, velocity, interface_flags, block_links, deck_node, mode_shapes, mobility):
    blocks, ext, _, height = fraction.shape
    devices = lax.axis_size("family")
    bits = devices.bit_length() - 1
    modes, nodes = mode_shapes.shape
    faces = 4 * blocks
    dims = (blocks, ext, height, bits)
    f32 = jnp.float32
    vmem = pl.BlockSpec(memory_space=pltpu.VMEM)
    smem = pl.BlockSpec(memory_space=pltpu.SMEM)
    hbm = pl.BlockSpec(memory_space=pltpu.HBM)
    params = pltpu.CompilerParams(vmem_limit_bytes=24 * MIB)
    flat_node = deck_node.reshape(blocks * ext, ext)
    packed = pl.pallas_call(
        functools.partial(pack_kernel, dims),
        out_shape=[pltpu.VMEM((CAP, 3, ext, height), f32)] * bits
        + [
            pltpu.VMEM((8, LANES), f32),
            pltpu.SMEM((bits * CAP,), jnp.int32),
            pltpu.VMEM(fraction.shape, f32),
            pltpu.VMEM(velocity.shape, jnp.bfloat16),
        ],
        in_specs=[smem, hbm, hbm, hbm, hbm],
        out_specs=[vmem] * (bits + 1) + [smem, vmem, vmem],
        scratch_shapes=[
            pltpu.VMEM((blocks * 2 * ext * 8, height), f32),
            pltpu.VMEM((2 * nodes // LANES, ext * height), jnp.bfloat16),
            pltpu.VMEM((LANES, ext * height), jnp.bfloat16),
            pltpu.VMEM((blocks * ext, ext), jnp.int32),
            pltpu.VMEM((modes, nodes), f32),
            pltpu.SMEM((bits,), jnp.int32),
            pltpu.SMEM((bits,), jnp.int32),
            pltpu.SMEM((bits * CAP,), jnp.int32),
            pltpu.SemaphoreType.DMA((2, blocks)),
            pltpu.SemaphoreType.DMA((2,)),
        ],
        compiler_params=params,
        name="pack",
    )(*(in_hbm(x) for x in (jnp.transpose(block_links, (2, 0, 1)), flat_node, mode_shapes, fraction, velocity)))
    outgoing, (red, got, fill, vel) = packed[:bits], packed[bits:]
    received = [None] * bits
    for k in reversed(range(bits)):
        received[k] = swapped(outgoing[k], "family", k)
    is_top = lax.broadcasted_iota(jnp.int32, red.shape, 1) == modes // 8
    for k in range(bits):
        other = swapped(red, "family", k)
        red = jnp.where(is_top, jnp.maximum(red, other), red + other)
    cells, flow = shift_tables(height)
    base, rate, rim, top = pl.pallas_call(
        functools.partial(rates_kernel, dims),
        out_shape=[
            jax.ShapeDtypeStruct(fraction.shape, f32),
            jax.ShapeDtypeStruct(fraction.shape, f32),
            jax.ShapeDtypeStruct((faces, 5, ext, height), f32),
            jax.ShapeDtypeStruct((ext, height), f32),
        ],
        in_specs=[vmem] * 6,
        out_specs=[vmem] * 4,
        scratch_shapes=[
            pltpu.VMEM((2 * ext * 8, height), f32),
            pltpu.VMEM((ext, ext, height), f32),
        ],
        compiler_params=params,
        cost_estimate=pl.CostEstimate(flops=80 * fraction.size, bytes_accessed=20 * fraction.size, transcendentals=0),
        name="rates",
    )(jnp.asarray(cells, jnp.bfloat16), jnp.asarray(flow, jnp.bfloat16), fill, vel, fraction_start, interface_flags)
    updated, deck = pl.pallas_call(
        functools.partial(final_kernel, dims, devices),
        out_shape=[
            jax.ShapeDtypeStruct(fraction.shape, f32),
            jax.ShapeDtypeStruct((blocks * ext, ext), f32),
        ],
        in_specs=[smem] + [vmem] * (8 + bits),
        out_specs=[hbm, vmem],
        scratch_shapes=[
            pltpu.VMEM((faces, 3, ext, height), f32),
            pltpu.VMEM((blocks, ext, ext, height), f32),
            pltpu.SemaphoreType.DMA((blocks,)),
        ],
        compiler_params=params,
        name="finish",
    )(got, mobility.reshape(1, modes), flat_node, mode_shapes, red, base, rate, rim, top, *received)
    return updated, deck.reshape(blocks, ext, ext)


def solution(mesh):
    in_specs = (
        P(("groups", "family"), None, None, None),
        P(("groups", "family"), None, None, None),
        P(("groups", "family"), None, None, None, None),
        P(("groups", "family"), None, None, None),
        P("family", None, None),
        P("family", None, None),
        P(),
        P(),
    )
    out_specs = (P(("groups", "family"), None, None, None), P(("groups", "family"), None, None))
    return jax.shard_map(local, mesh=mesh, in_specs=in_specs, out_specs=out_specs, check_vma=False)
```

```python
import functools
import math

import jax
import jax.numpy as jnp
import numpy as np
from jax import lax
from jax.experimental import pallas as pl
from jax.experimental.pallas import tpu as pltpu
from jax.sharding import PartitionSpec as P

CAP = 4
CFL_NUMBER = 0.4
SHARPEN = 2.0
DECK_GAIN = 0.15
EPSILON = 1e-06
LANES = 128
MIB = 1024 * 1024
RATES_BYTES = 10 * MIB


def crossed(x, axis, mask):
    return lax.ppermute(x, axis, [(i, i ^ mask) for i in range(lax.axis_size(axis))])


def limited(first, second):
    return jnp.maximum(jnp.minimum(second, jnp.maximum(first, 0.0)), jnp.minimum(first, 0.0))


def set_bits(x):
    x = x - ((x >> 1) & 0x5555)
    x = (x & 0x3333) + ((x >> 2) & 0x3333)
    x = (x + (x >> 4)) & 0x0F0F
    return (x + (x >> 8)) & 0x1F


def route(links, me, blocks, bits, count, mask, sent, got):
    for k in range(bits):
        count[k] = 0
        mask[k] = 0
        for s in range(CAP):
            sent[k * CAP + s] = 0
            got[k * CAP + s] = -1
    shift = blocks.bit_length() - 1
    found = []
    for face in range(4 * blocks):
        b, t = face // 4, face % 4
        partner = links[0, b, t]
        differ = (partner >> shift) ^ me
        k = jnp.int32(0)
        for q in range(1, bits):
            k = k + (differ >= (1 << q)).astype(jnp.int32)
        r = count[k]
        count[k] = r + 1
        sent[k * CAP + r] = face
        source = (partner & (blocks - 1)) * 4 + links[1, b, t]
        mask[k] = mask[k] | (jnp.int32(1) << source)
        found.append((k, source))
    for face, (k, source) in enumerate(found):
        rank = set_bits(mask[k] & ((jnp.int32(1) << source) - 1))
        got[k * CAP + rank] = 2 * face + links[2, face // 4, face % 4]


def pack_kernel(dims, tiles, links, fill, vel, *rest):
    blocks, ext, height, bits = dims
    outs = rest[:bits]
    got, top_at, edge, count, mask, sent = rest[bits:]
    top_at[...] = (lax.broadcasted_iota(jnp.int32, top_at.shape, 1) == tiles).astype(jnp.float32)
    area = ext * ext
    route(links, lax.axis_index("family"), blocks, bits, count, mask, sent, got)
    for b in range(blocks):
        for side in range(2):
            x = vel[b, 1, :, side * (ext - 16) : side * (ext - 16) + 16, :].astype(jnp.float32)[:, 8 * side : 8 * side + 8]
            edge[pl.ds((b * 2 + side) * ext * 8, ext * 8), :] = x.reshape(ext * 8, height)
    rows = fill.reshape(blocks * area, height)
    for k in range(bits):
        for s in range(CAP):
            face = sent[k * CAP + s]
            b, t = face >> 2, face & 3
            side = t & 1
            sign = (2 * side - 1).astype(jnp.float32)
            near = side * (ext - 1)
            after = near + 1 - 2 * side

            @pl.when(t < 2)
            def _():
                outs[k][s, 0] = fill[b, near]
                outs[k][s, 1] = fill[b, after]
                outs[k][s, 2] = vel[b, 0, near].astype(jnp.float32) * sign

            @pl.when(t >= 2)
            def _():
                outs[k][s, 0] = rows[pl.ds(b * area + near, ext, stride=ext), :]
                outs[k][s, 1] = rows[pl.ds(b * area + after, ext, stride=ext), :]
                outs[k][s, 2] = edge[pl.ds((b * 2 + side) * ext * 8 + side * 7, ext, stride=8), :] * sign


def reduce_kernel(dims, node_hbm, shapes_hbm, fill_hbm, vel_hbm, red_ref, fill, vel, left, right, node_ref, shapes_ref, sems, late):
    blocks, ext, height, bits = dims
    early = pltpu.make_async_copy(node_hbm, node_ref, late.at[0])
    early.start()
    fill_copies, vel_copies = [], []
    for b in range(blocks):
        fill_copies.append(pltpu.make_async_copy(fill_hbm.at[b], fill.at[b], sems.at[0, b]))
        vel_copies.append(pltpu.make_async_copy(vel_hbm.at[b], vel.at[b], sems.at[1, b]))
        vel_copies[b].start()
        fill_copies[b].start()
    last = pltpu.make_async_copy(shapes_hbm, shapes_ref, late.at[1])
    last.start()
    early.wait()
    node = node_ref[...].T
    high, low = node >> 7, node & 127
    low_at = lax.broadcasted_iota(jnp.int32, (LANES, height), 0)
    for j in range(ext):
        right[:, j * height : (j + 1) * height] = jnp.where(low_at == low[j : j + 1], 1.0, 0.0).astype(jnp.bfloat16)
    lane = lax.broadcasted_iota(jnp.int32, (ext, height), 1)
    pressure = jnp.zeros((ext, height), jnp.float32)
    speed = jnp.zeros((ext, height), jnp.bfloat16)
    for b in range(blocks):
        vel_copies[b].wait()
        fill_copies[b].wait()

        def step(i, carry):
            pressure, speed = carry
            up = vel[b, 2, i]
            speed = jnp.maximum(speed, jnp.abs(vel[b, 0, i]))
            speed = jnp.maximum(speed, jnp.abs(vel[b, 1, i]))
            speed = jnp.maximum(speed, jnp.abs(up))
            up = up.astype(jnp.float32)
            push = fill[b, i] * (1.0 + up * up)
            at = b * ext + i
            pressure = jnp.where(lane == at, pltpu.roll(push, at + 1, 1), pressure)
            return pressure, speed

        pressure, speed = lax.fori_loop(0, ext, step, (pressure, speed), unroll=True)
    last.wait()
    groups = shapes_ref.shape[1] // LANES
    first = pressure.astype(jnp.bfloat16).astype(jnp.float32)
    second = pressure - first
    high_at = lax.broadcasted_iota(jnp.int32, (groups, height), 0)
    for j in range(ext):
        same = high_at == high[j : j + 1]
        cols = pl.ds(j * height, height)
        left[0:groups, cols] = jnp.where(same, first[j : j + 1], 0.0).astype(jnp.bfloat16)
        left[groups : 2 * groups, cols] = jnp.where(same, second[j : j + 1], 0.0).astype(jnp.bfloat16)
    nodal = lax.dot_general(left[...], right[...], (((1,), (1,)), ((), ())), preferred_element_type=jnp.float32)
    nodal = nodal[:groups] + nodal[groups:]
    lane8 = lax.broadcasted_iota(jnp.int32, (8, LANES), 1)
    tiles = shapes_ref.shape[0] // 8
    top = jnp.max(jnp.max(speed.astype(jnp.float32), axis=0, keepdims=True), axis=1, keepdims=True)
    red = jnp.where(lane8 == tiles, top, 0.0)
    for t in range(tiles):
        total = jnp.zeros((8, LANES), jnp.float32)
        for g in range(groups):
            total = total + shapes_ref[8 * t : 8 * t + 8, g * LANES : (g + 1) * LANES] * nodal[g : g + 1]
        red = jnp.where(lane8 == t, jnp.sum(total, axis=1, keepdims=True), red)
    red_ref[...] = red


def shift_tables(height):
    k = np.arange(height)
    eye = np.eye(height, dtype=np.float32)
    nxt = np.eye(height, k=-1, dtype=np.float32)
    nxt2 = np.eye(height, k=-2, dtype=np.float32)
    prv = np.eye(height, k=1, dtype=np.float32)
    before = 0.5 * (eye - prv); before[:, 0] = 0
    step = 0.5 * (nxt - eye); step[:, -1] = 0
    after = 0.5 * (nxt2 - nxt); after[:, -2:] = 0
    cells = np.concatenate([before, step, after, nxt], 1)
    flow = nxt + eye; flow[:, -1] = 0
    return np.concatenate([cells, cells], 0), flow
def rates_kernel(dims, cells_ref, flow_ref, fill, vel, start, flag, base_ref, rate_ref, rim_ref, top_ref, edge, lift):
    blocks, ext, height, bits = dims
    area = ext * ext
    lane = lax.broadcasted_iota(jnp.int32, (ext, height), 1)
    row = lax.broadcasted_iota(jnp.int32, (ext, height), 0)
    open_row = (row >= 1) & (row <= ext - 3)
    rows = fill.reshape(blocks * area, height)
    layers = 8
    size = layers * ext
    top = jnp.zeros((ext, height), jnp.float32)
    def block(b, top):

        def column(c, carry):
            x = fill[b, pl.ds(c * layers, layers)].reshape(size, height)
            u = vel[b, 2, pl.ds(c * layers, layers)].reshape(size, height)
            high = x.astype(jnp.bfloat16)
            low = (x - high.astype(jnp.float32)).astype(jnp.bfloat16)
            y = jnp.dot(jnp.concatenate([high, low], 1), cells_ref[...], preferred_element_type=jnp.float32)
            v = jnp.dot(u, flow_ref[...], preferred_element_type=jnp.float32)
            step = y[:, height : 2 * height]
            ahead = x + limited(step, y[:, :height])
            behind = y[:, 3 * height :] - limited(step, y[:, 2 * height : 3 * height])
            lift[pl.ds(c * layers, layers)] = (v * jnp.where(v > 0.0, ahead, behind)).reshape(layers, ext, height)
            return carry

        lax.fori_loop(0, ext // layers, column, 0, unroll=True)

        def own(i, f, h):
            flux = lift[i]
            rate = pltpu.roll(flux, 1, 1) - flux
            step = pltpu.roll(h, ext - 1, 0) - h
            slope = limited(pltpu.roll(step, 1, 0), step)
            u = vel[b, 1, i].astype(jnp.float32)
            v = u + pltpu.roll(u, ext - 1, 0)
            v = jnp.where(open_row, v, 0.0)
            flux = v * jnp.where(v > 0.0, f + slope, pltpu.roll(f - slope, ext - 1, 0))
            rate = rate + (pltpu.roll(flux, 1, 0) - flux)
            sharp = (f * (1.0 - f)) * ((4.0 * SHARPEN) * f - 2.0 * SHARPEN)
            rate = rate + jnp.where(flag[b, i] != 0, sharp, 0.0)
            base_ref[b, i] = 0.75 * start[b, i] + 0.25 * f
            return rate

        def picked(i, f, top):
            at = b * ext + i
            return jnp.where(lane == at, pltpu.roll(f, at + 1, 1), top)

        f0 = fill[b, 0]
        rate_ref[b, 0] = own(0, f0, 0.5 * f0)
        top = picked(0, f0, top)
        f1 = fill[b, 1]
        h1 = 0.5 * f1
        rate1 = own(1, f1, h1)
        top = picked(1, f1, top)
        f2 = fill[b, 2]
        h2 = 0.5 * f2
        step = h2 - h1
        ahead = f1 + limited(h1 - 0.5 * f0, step)

        def layer(i, carry):
            f, h, step_before, ahead, flux_before, u_before, rate_before, top = carry
            f_next = fill[b, i + 1]
            h_next = 0.5 * f_next
            step = h_next - h
            slope = limited(step_before, step)
            u = vel[b, 0, i].astype(jnp.float32)
            v = u_before + u
            flux = v * jnp.where(v > 0.0, ahead, f - slope)
            rate_ref[b, i - 1] = rate_before + (flux_before - flux)
            return f_next, h_next, step, f + slope, flux, u, own(i, f, h), picked(i, f, top)

        carry = (f2, h2, step, ahead, jnp.zeros_like(f0), vel[b, 0, 1].astype(jnp.float32), rate1, top)
        carry = lax.fori_loop(2, ext - 1, layer, carry, unroll=True)
        f, h, _, _, flux, _, rate, top = carry
        rate_ref[b, ext - 2] = rate + flux
        rate_ref[b, ext - 1] = own(ext - 1, f, h)
        top = picked(ext - 1, f, top)

        for side in range(2):
            x = vel[b, 1, :, side * (ext - 16) : side * (ext - 16) + 16, :].astype(jnp.float32)[:, 8 * side : 8 * side + 8]
            edge[pl.ds(side * ext * 8, ext * 8), :] = x.reshape(ext * 8, height)
        for t in range(4):
            side = t % 2
            sign = 1.0 - 2.0 * side
            at = [side * (ext - 1) + d * (1 - 2 * side) for d in range(3)]
            if t < 2:
                cells = [fill[b, i] for i in at]
                flows = [vel[b, 0, i].astype(jnp.float32) * sign for i in at[:2]]
            else:
                cells = [rows[pl.ds(b * area + j, ext, stride=ext), :] for j in at]
                flows = [edge[pl.ds(side * ext * 8 + j % 8, ext, stride=8), :] * sign for j in at[:2]]
            step = 0.5 * (cells[1] - cells[0])
            slope = limited(step, 0.5 * (cells[2] - cells[1]))
            rim_ref[4 * b + t, 0] = cells[0]
            rim_ref[4 * b + t, 1] = step
            rim_ref[4 * b + t, 2] = cells[1] - slope
            rim_ref[4 * b + t, 3] = flows[0]
            rim_ref[4 * b + t, 4] = flows[0] + flows[1]
        return top
    top_ref[...] = lax.fori_loop(0, blocks, block, top)


def update_kernel(dims, devices, mobility_ref, node_ref, shapes_ref, red_ref, base_ref, rate_ref, top_ref, out, deck_ref, scale_ref):
    blocks, ext, height, bits = dims
    area = ext * ext
    tiles = shapes_ref.shape[0] // 8
    groups = shapes_ref.shape[1] // LANES
    red = red_ref[...]
    time_step = CFL_NUMBER / (red[0:1, tiles : tiles + 1] + EPSILON)
    eighth = 0.125 * time_step
    scale = math.sqrt(shapes_ref.shape[1]) / (blocks * devices * area)
    lane8 = lax.broadcasted_iota(jnp.int32, (8, LANES), 1)
    sub8 = lax.broadcasted_iota(jnp.int32, (8, LANES), 0)
    mobility = mobility_ref[...]
    sums = [jnp.zeros((8, LANES), jnp.float32) for _ in range(groups)]
    width = mobility.shape[1]
    for t in range(tiles):
        pick = lax.broadcasted_iota(jnp.int32, (8, width), 1) == 8 * t + lax.broadcasted_iota(jnp.int32, (8, width), 0)
        gain = jnp.sum(jnp.where(pick, mobility, 0.0), axis=1, keepdims=True)
        speed = jnp.broadcast_to(gain * (red[:, t : t + 1] * scale), (8, LANES))
        for g in range(groups):
            sums[g] = sums[g] + shapes_ref[8 * t : 8 * t + 8, g * LANES : (g + 1) * LANES] * speed
    node = node_ref[...].T
    high, low = node >> 7, node & 127
    deck = jnp.zeros((ext, height), jnp.float32)
    for g in range(groups):
        line = jnp.broadcast_to(jnp.sum(sums[g], axis=0, keepdims=True), (8, LANES))
        values = [jnp.take_along_axis(line, low[8 * q : 8 * q + 8], axis=1) for q in range(ext // 8)]
        deck = jnp.where(high == g, jnp.concatenate(values, 0), deck)
    deck = jnp.tanh(DECK_GAIN * deck)
    deck_ref[...] = deck.T
    lane = lax.broadcasted_iota(jnp.int32, (ext, height), 1)
    last_lane = lane == height - 1
    deck = deck * (2.0 * eighth) * top_ref[...]

    scale_ref[...] = jnp.broadcast_to(eighth, scale_ref.shape)
    for b in range(blocks):

        def layer(i, carry):
            at = b * ext + i
            lid = jnp.where(last_lane, pltpu.roll(deck, height - 1 - at, 1), 0.0)
            out[b, i] = base_ref[b, i] + eighth * rate_ref[b, i] - lid
            return carry

        lax.fori_loop(0, ext, layer, 0, unroll=True)


def final_kernel(dims, got, scale_ref, rim_ref, part_in, *rest):
    blocks, ext, height, bits = dims
    ghosts = rest[:bits]
    out_hbm, part, ghost, sems = rest[bits:]
    area = ext * ext
    turned = 7 - lax.broadcasted_iota(jnp.int32, (8, height), 0)
    for k in range(bits):
        for s in range(CAP):
            code = got[k * CAP + s]
            face, flip = code >> 1, code & 1

            @pl.when((code >= 0) & (flip == 0))
            def _():
                ghost[face] = ghosts[k][s]

            @pl.when((code >= 0) & (flip == 1))
            def _():
                for c in range(3):
                    for q in range(ext // 8):
                        x = ghosts[k][s, c, ext - 8 - 8 * q : ext - 8 * q, :]
                        ghost[face, c, 8 * q : 8 * q + 8, :] = jnp.take_along_axis(x, turned, axis=0)

    rows = part.reshape(blocks * area, height)
    eighth = scale_ref[0:1, 0:1]
    copies = []
    for b in range(blocks):
        for t in range(4):
            face = 4 * b + t
            side = t % 2
            near = side * (ext - 1)
            after = near + 1 - 2 * side
            g0, g1, gv = ghost[face, 0], ghost[face, 1], ghost[face, 2]
            c0, step1, behind1, u0, v1 = (rim_ref[face, q] for q in range(5))
            step0 = 0.5 * (c0 - g0)
            ghost_slope = limited(step0, 0.5 * (g0 - g1))
            slope = limited(step0, step1)
            v0 = gv + u0
            flux0 = v0 * jnp.where(v0 > 0.0, g0 + ghost_slope, c0 - slope)
            flux1 = v1 * jnp.where(v1 > 0.0, c0 + slope, behind1)
            for where, add in ((near, eighth * (flux0 - flux1)), (after, eighth * flux1)):
                if t < 2:
                    part[b, where] = part[b, where] + add
                else:
                    line = pl.ds(b * area + where, ext, stride=ext)
                    rows[line, :] = rows[line, :] + add
        copy = pltpu.make_async_copy(part.at[b], out_hbm.at[b], sems.at[b])
        copy.start()
        copies.append(copy)
    for copy in copies:
        copy.wait()


def in_hbm(x):
    return pltpu.with_memory_space_constraint(x, pltpu.HBM)


def local(fraction, fraction_start, velocity, interface_flags, block_links, deck_node, mode_shapes, mobility):
    blocks, ext, _, height = fraction.shape
    devices = lax.axis_size("family")
    bits = devices.bit_length() - 1
    modes, nodes = mode_shapes.shape
    faces = 4 * blocks
    dims = (blocks, ext, height, bits)
    f32 = jnp.float32
    vmem = pl.BlockSpec(memory_space=pltpu.VMEM)
    smem = pl.BlockSpec(memory_space=pltpu.SMEM)
    hbm = pl.BlockSpec(memory_space=pltpu.HBM)
    params = pltpu.CompilerParams(vmem_limit_bytes=24 * MIB)
    flat_node = deck_node.reshape(blocks * ext, ext)
    tables = [jnp.asarray(x, jnp.bfloat16) for x in shift_tables(height)]
    red, fill, vel = pl.pallas_call(
        functools.partial(reduce_kernel, dims),
        out_shape=[pltpu.VMEM((8, LANES), f32), pltpu.VMEM(fraction.shape, f32), pltpu.VMEM(velocity.shape, jnp.bfloat16)],
        in_specs=[hbm] * 4,
        out_specs=[vmem] * 3,
        scratch_shapes=[
            pltpu.VMEM((2 * nodes // LANES, ext * height), jnp.bfloat16),
            pltpu.VMEM((LANES, ext * height), jnp.bfloat16),
            pltpu.VMEM((blocks * ext, ext), jnp.int32),
            pltpu.VMEM((modes, nodes), f32),
            pltpu.SemaphoreType.DMA((2, blocks)),
            pltpu.SemaphoreType.DMA((2,)),
        ],
        compiler_params=params,
        name="reduce",
    )(*(in_hbm(x) for x in (flat_node, mode_shapes, fraction, velocity)))
    packed = pl.pallas_call(
        functools.partial(pack_kernel, dims, modes // 8),
        out_shape=[pltpu.VMEM((CAP, 3, ext, height), f32)] * bits + [pltpu.SMEM((bits * CAP,), jnp.int32), pltpu.VMEM((8, LANES), f32)],
        in_specs=[smem, vmem, vmem],
        out_specs=[vmem] * bits + [smem, vmem],
        scratch_shapes=[
            pltpu.VMEM((blocks * 2 * ext * 8, height), f32),
            pltpu.SMEM((bits,), jnp.int32),
            pltpu.SMEM((bits,), jnp.int32),
            pltpu.SMEM((bits * CAP,), jnp.int32),
        ],
        compiler_params=params,
        cost_estimate=pl.CostEstimate(flops=0, bytes_accessed=2 * MIB, transcendentals=0),
        name="pack",
    )(jnp.transpose(block_links, (2, 0, 1)), fill, vel)
    outgoing, (got, top_at) = packed[:bits], packed[bits:]
    received = [crossed(outgoing[k], "family", 1 << k) for k in range(bits)]
    marks = [(lax.broadcasted_iota(jnp.int32, red.shape, 1) == modes // 8).astype(f32)] * bits
    marks[1] = top_at
    for k in range(bits):
        other = crossed(red, "family", 1 << k)
        red = jnp.where(marks[k] > 0.0, jnp.maximum(red, other), red + other)
    base, rate, rim, top = pl.pallas_call(
        functools.partial(rates_kernel, dims),
        out_shape=[
            jax.ShapeDtypeStruct(fraction.shape, f32),
            jax.ShapeDtypeStruct(fraction.shape, f32),
            jax.ShapeDtypeStruct((faces, 5, ext, height), f32),
            jax.ShapeDtypeStruct((ext, height), f32),
        ],
        in_specs=[vmem] * 6,
        out_specs=[vmem] * 4,
        scratch_shapes=[
            pltpu.VMEM((2 * ext * 8, height), f32),
            pltpu.VMEM((ext, ext, height), f32),
        ],
        compiler_params=params,
        cost_estimate=pl.CostEstimate(flops=80 * fraction.size, bytes_accessed=RATES_BYTES, transcendentals=0),
        name="rates",
    )(*tables, fill, vel, fraction_start, interface_flags)
    part, deck, step = pl.pallas_call(
        functools.partial(update_kernel, dims, devices),
        out_shape=[
            pltpu.VMEM(fraction.shape, f32),
            jax.ShapeDtypeStruct((blocks * ext, ext), f32),
            pltpu.VMEM((8, LANES), f32),
        ],
        in_specs=[vmem] * 7,
        out_specs=[vmem] * 3,
        compiler_params=params,
        name="update",
    )(mobility.reshape(1, modes), flat_node, mode_shapes, red, base, rate, top)
    updated, _ = pl.pallas_call(
        functools.partial(final_kernel, dims),
        out_shape=[jax.ShapeDtypeStruct(fraction.shape, f32), pltpu.VMEM(fraction.shape, f32)],
        in_specs=[smem] + [vmem] * (3 + bits),
        out_specs=[hbm, vmem],
        scratch_shapes=[
            pltpu.VMEM((faces, 3, ext, height), f32),
            pltpu.SemaphoreType.DMA((blocks,)),
        ],
        input_output_aliases={3: 1},
        compiler_params=params,
        name="finish",
    )(got, step, rim, part, *received)
    return updated, deck.reshape(blocks, ext, ext)


def solution(mesh):
    in_specs = (
        P(("groups", "family"), None, None, None),
        P(("groups", "family"), None, None, None),
        P(("groups", "family"), None, None, None, None),
        P(("groups", "family"), None, None, None),
        P("family", None, None),
        P("family", None, None),
        P(),
        P(),
    )
    out_specs = (P(("groups", "family"), None, None, None), P(("groups", "family"), None, None))
    return jax.shard_map(local, mesh=mesh, in_specs=in_specs, out_specs=out_specs, check_vma=False)
```

```python
import functools
import math

import jax
import jax.numpy as jnp
import numpy as np
from jax import lax
from jax.experimental import pallas as pl
from jax.experimental.pallas import tpu as pltpu
from jax.sharding import PartitionSpec as P

CAP = 4
CFL_NUMBER = 0.4
SHARPEN = 2.0
DECK_GAIN = 0.15
EPSILON = 1e-06
LANES = 128
MIB = 1024 * 1024
RATES_BYTES = 10 * MIB


def crossed(x, axis, mask):
    return lax.ppermute(x, axis, [(i, i ^ mask) for i in range(lax.axis_size(axis))])


def limited(first, second):
    return jnp.maximum(jnp.minimum(second, jnp.maximum(first, 0.0)), jnp.minimum(first, 0.0))


def set_bits(x):
    x = x - ((x >> 1) & 0x5555)
    x = (x & 0x3333) + ((x >> 2) & 0x3333)
    x = (x + (x >> 4)) & 0x0F0F
    return (x + (x >> 8)) & 0x1F


def route(links, me, blocks, bits, count, mask, sent, got):
    for k in range(bits):
        count[k] = 0
        mask[k] = 0
        for s in range(CAP):
            sent[k * CAP + s] = 0
            got[k * CAP + s] = -1
    shift = blocks.bit_length() - 1
    found = []
    for face in range(4 * blocks):
        b, t = face // 4, face % 4
        partner = links[0, b, t]
        differ = (partner >> shift) ^ me
        k = jnp.int32(0)
        for q in range(1, bits):
            k = k + (differ >= (1 << q)).astype(jnp.int32)
        r = count[k]
        count[k] = r + 1
        sent[k * CAP + r] = face
        source = (partner & (blocks - 1)) * 4 + links[1, b, t]
        mask[k] = mask[k] | (jnp.int32(1) << source)
        found.append((k, source))
    for face, (k, source) in enumerate(found):
        rank = set_bits(mask[k] & ((jnp.int32(1) << source) - 1))
        got[k * CAP + rank] = 2 * face + links[2, face // 4, face % 4]


def pack_kernel(dims, tiles, links, fill, vel, *rest):
    blocks, ext, height, bits = dims
    outs = rest[:bits]
    got, top_at, edge, count, mask, sent = rest[bits:]
    top_at[...] = (lax.broadcasted_iota(jnp.int32, top_at.shape, 1) == tiles).astype(jnp.float32)
    area = ext * ext
    route(links, lax.axis_index("family"), blocks, bits, count, mask, sent, got)
    for b in range(blocks):
        for side in range(2):
            x = vel[b, 1, :, side * (ext - 16) : side * (ext - 16) + 16, :].astype(jnp.float32)[:, 8 * side : 8 * side + 8]
            edge[pl.ds((b * 2 + side) * ext * 8, ext * 8), :] = x.reshape(ext * 8, height)
    rows = fill.reshape(blocks * area, height)
    for k in range(bits):
        for s in range(CAP):
            face = sent[k * CAP + s]
            b, t = face >> 2, face & 3
            side = t & 1
            sign = (2 * side - 1).astype(jnp.float32)
            near = side * (ext - 1)
            after = near + 1 - 2 * side

            @pl.when(t < 2)
            def _():
                outs[k][s, 0] = fill[b, near]
                outs[k][s, 1] = fill[b, after]
                outs[k][s, 2] = vel[b, 0, near].astype(jnp.float32) * sign

            @pl.when(t >= 2)
            def _():
                outs[k][s, 0] = rows[pl.ds(b * area + near, ext, stride=ext), :]
                outs[k][s, 1] = rows[pl.ds(b * area + after, ext, stride=ext), :]
                outs[k][s, 2] = edge[pl.ds((b * 2 + side) * ext * 8 + side * 7, ext, stride=8), :] * sign


def reduce_kernel(dims, node_hbm, shapes_hbm, fill_hbm, vel_hbm, red_ref, fill, vel, left, right, node_ref, shapes_ref, sems, late):
    blocks, ext, height, bits = dims
    early = pltpu.make_async_copy(node_hbm, node_ref, late.at[0])
    early.start()
    fill_copies, vel_copies = [], []
    for b in range(blocks):
        fill_copies.append(pltpu.make_async_copy(fill_hbm.at[b], fill.at[b], sems.at[0, b]))
        vel_copies.append(pltpu.make_async_copy(vel_hbm.at[b], vel.at[b], sems.at[1, b]))
        vel_copies[b].start()
        fill_copies[b].start()
    last = pltpu.make_async_copy(shapes_hbm, shapes_ref, late.at[1])
    last.start()
    early.wait()
    node = node_ref[...].T
    high, low = node >> 7, node & 127
    low_at = lax.broadcasted_iota(jnp.int32, (LANES, height), 0)
    for j in range(ext):
        right[:, j * height : (j + 1) * height] = jnp.where(low_at == low[j : j + 1], 1.0, 0.0).astype(jnp.bfloat16)
    lane = lax.broadcasted_iota(jnp.int32, (ext, height), 1)
    pressure = jnp.zeros((ext, height), jnp.float32)
    speed = jnp.zeros((ext, height), jnp.bfloat16)
    for b in range(blocks):
        vel_copies[b].wait()
        fill_copies[b].wait()

        def step(i, carry):
            pressure, speed = carry
            up = vel[b, 2, i]
            speed = jnp.maximum(speed, jnp.abs(vel[b, 0, i]))
            speed = jnp.maximum(speed, jnp.abs(vel[b, 1, i]))
            speed = jnp.maximum(speed, jnp.abs(up))
            up = up.astype(jnp.float32)
            push = fill[b, i] * (1.0 + up * up)
            at = b * ext + i
            pressure = jnp.where(lane == at, pltpu.roll(push, at + 1, 1), pressure)
            return pressure, speed

        pressure, speed = lax.fori_loop(0, ext, step, (pressure, speed), unroll=True)
    last.wait()
    groups = shapes_ref.shape[1] // LANES
    first = pressure.astype(jnp.bfloat16).astype(jnp.float32)
    second = pressure - first
    high_at = lax.broadcasted_iota(jnp.int32, (groups, height), 0)
    for j in range(ext):
        same = high_at == high[j : j + 1]
        cols = pl.ds(j * height, height)
        left[0:groups, cols] = jnp.where(same, first[j : j + 1], 0.0).astype(jnp.bfloat16)
        left[groups : 2 * groups, cols] = jnp.where(same, second[j : j + 1], 0.0).astype(jnp.bfloat16)
    nodal = lax.dot_general(left[...], right[...], (((1,), (1,)), ((), ())), preferred_element_type=jnp.float32)
    nodal = nodal[:groups] + nodal[groups:]
    lane8 = lax.broadcasted_iota(jnp.int32, (8, LANES), 1)
    tiles = shapes_ref.shape[0] // 8
    top = jnp.max(jnp.max(speed.astype(jnp.float32), axis=0, keepdims=True), axis=1, keepdims=True)
    red = jnp.where(lane8 == tiles, top, 0.0)
    for t in range(tiles):
        total = jnp.zeros((8, LANES), jnp.float32)
        for g in range(groups):
            total = total + shapes_ref[8 * t : 8 * t + 8, g * LANES : (g + 1) * LANES] * nodal[g : g + 1]
        red = jnp.where(lane8 == t, jnp.sum(total, axis=1, keepdims=True), red)
    red_ref[...] = red


def shift_tables(height):
    k = np.arange(height)
    eye = np.eye(height, dtype=np.float32)
    nxt = np.eye(height, k=-1, dtype=np.float32)
    nxt2 = np.eye(height, k=-2, dtype=np.float32)
    prv = np.eye(height, k=1, dtype=np.float32)
    before = 0.5 * (eye - prv); before[:, 0] = 0
    step = 0.5 * (nxt - eye); step[:, -1] = 0
    after = 0.5 * (nxt2 - nxt); after[:, -2:] = 0
    cells = np.concatenate([before, step, after, nxt], 1)
    flow = nxt + eye; flow[:, -1] = 0
    return np.concatenate([cells, cells], 0), flow
def rates_kernel(dims, cells_ref, flow_ref, fill, vel, start, flag, base_ref, rate_ref, rim_ref, top_ref, edge, lift):
    blocks, ext, height, bits = dims
    area = ext * ext
    lane = lax.broadcasted_iota(jnp.int32, (ext, height), 1)
    row = lax.broadcasted_iota(jnp.int32, (ext, height), 0)
    open_row = (row >= 1) & (row <= ext - 3)
    rows = fill.reshape(blocks * area, height)
    layers = 8
    size = layers * ext
    top = jnp.zeros((ext, height), jnp.float32)
    def block(b, top):

        def column(c, carry):
            x = fill[b, pl.ds(c * layers, layers)].reshape(size, height)
            u = vel[b, 2, pl.ds(c * layers, layers)].reshape(size, height)
            high = x.astype(jnp.bfloat16)
            low = (x - high.astype(jnp.float32)).astype(jnp.bfloat16)
            y = jnp.dot(jnp.concatenate([high, low], 1), cells_ref[...], preferred_element_type=jnp.float32)
            v = jnp.dot(u, flow_ref[...], preferred_element_type=jnp.float32)
            step = y[:, height : 2 * height]
            ahead = x + limited(step, y[:, :height])
            behind = y[:, 3 * height :] - limited(step, y[:, 2 * height : 3 * height])
            lift[pl.ds(c * layers, layers)] = (v * jnp.where(v > 0.0, ahead, behind)).reshape(layers, ext, height)
            return carry

        lax.fori_loop(0, ext // layers, column, 0, unroll=True)

        def own(i, f, h):
            flux = lift[i]
            rate = pltpu.roll(flux, 1, 1) - flux
            step = pltpu.roll(h, ext - 1, 0) - h
            slope = limited(pltpu.roll(step, 1, 0), step)
            u = vel[b, 1, i].astype(jnp.float32)
            v = u + pltpu.roll(u, ext - 1, 0)
            v = jnp.where(open_row, v, 0.0)
            flux = v * jnp.where(v > 0.0, f + slope, pltpu.roll(f - slope, ext - 1, 0))
            rate = rate + (pltpu.roll(flux, 1, 0) - flux)
            sharp = (f * (1.0 - f)) * ((4.0 * SHARPEN) * f - 2.0 * SHARPEN)
            rate = rate + jnp.where(flag[b, i] != 0, sharp, 0.0)
            base_ref[b, i] = 0.75 * start[b, i] + 0.25 * f
            return rate

        def picked(i, f, top):
            at = b * ext + i
            return jnp.where(lane == at, pltpu.roll(f, at + 1, 1), top)

        f0 = fill[b, 0]
        rate_ref[b, 0] = own(0, f0, 0.5 * f0)
        top = picked(0, f0, top)
        f1 = fill[b, 1]
        h1 = 0.5 * f1
        rate1 = own(1, f1, h1)
        top = picked(1, f1, top)
        f2 = fill[b, 2]
        h2 = 0.5 * f2
        step = h2 - h1
        ahead = f1 + limited(h1 - 0.5 * f0, step)

        def layer(i, carry):
            f, h, step_before, ahead, flux_before, u_before, rate_before, top = carry
            f_next = fill[b, i + 1]
            h_next = 0.5 * f_next
            step = h_next - h
            slope = limited(step_before, step)
            u = vel[b, 0, i].astype(jnp.float32)
            v = u_before + u
            flux = v * jnp.where(v > 0.0, ahead, f - slope)
            rate_ref[b, i - 1] = rate_before + (flux_before - flux)
            return f_next, h_next, step, f + slope, flux, u, own(i, f, h), picked(i, f, top)

        carry = (f2, h2, step, ahead, jnp.zeros_like(f0), vel[b, 0, 1].astype(jnp.float32), rate1, top)
        carry = lax.fori_loop(2, ext - 1, layer, carry, unroll=True)
        f, h, _, _, flux, _, rate, top = carry
        rate_ref[b, ext - 2] = rate + flux
        rate_ref[b, ext - 1] = own(ext - 1, f, h)
        top = picked(ext - 1, f, top)

        for side in range(2):
            x = vel[b, 1, :, side * (ext - 16) : side * (ext - 16) + 16, :].astype(jnp.float32)[:, 8 * side : 8 * side + 8]
            edge[pl.ds(side * ext * 8, ext * 8), :] = x.reshape(ext * 8, height)
        for t in range(4):
            side = t % 2
            sign = 1.0 - 2.0 * side
            at = [side * (ext - 1) + d * (1 - 2 * side) for d in range(3)]
            if t < 2:
                cells = [fill[b, i] for i in at]
                flows = [vel[b, 0, i].astype(jnp.float32) * sign for i in at[:2]]
            else:
                cells = [rows[pl.ds(b * area + j, ext, stride=ext), :] for j in at]
                flows = [edge[pl.ds(side * ext * 8 + j % 8, ext, stride=8), :] * sign for j in at[:2]]
            step = 0.5 * (cells[1] - cells[0])
            slope = limited(step, 0.5 * (cells[2] - cells[1]))
            rim_ref[4 * b + t, 0] = cells[0]
            rim_ref[4 * b + t, 1] = step
            rim_ref[4 * b + t, 2] = cells[1] - slope
            rim_ref[4 * b + t, 3] = flows[0]
            rim_ref[4 * b + t, 4] = flows[0] + flows[1]
        return top
    top_ref[...] = lax.fori_loop(0, blocks, block, top)


def update_kernel(dims, devices, mobility_ref, node_ref, shapes_ref, red_ref, base_ref, rate_ref, top_ref, out, deck_ref, scale_ref):
    blocks, ext, height, bits = dims
    area = ext * ext
    tiles = shapes_ref.shape[0] // 8
    groups = shapes_ref.shape[1] // LANES
    red = red_ref[...]
    time_step = CFL_NUMBER / (red[0:1, tiles : tiles + 1] + EPSILON)
    eighth = 0.125 * time_step
    scale = math.sqrt(shapes_ref.shape[1]) / (blocks * devices * area)
    lane8 = lax.broadcasted_iota(jnp.int32, (8, LANES), 1)
    sub8 = lax.broadcasted_iota(jnp.int32, (8, LANES), 0)
    mobility = mobility_ref[...]
    sums = [jnp.zeros((8, LANES), jnp.float32) for _ in range(groups)]
    width = mobility.shape[1]
    for t in range(tiles):
        pick = lax.broadcasted_iota(jnp.int32, (8, width), 1) == 8 * t + lax.broadcasted_iota(jnp.int32, (8, width), 0)
        gain = jnp.sum(jnp.where(pick, mobility, 0.0), axis=1, keepdims=True)
        speed = jnp.broadcast_to(gain * (red[:, t : t + 1] * scale), (8, LANES))
        for g in range(groups):
            sums[g] = sums[g] + shapes_ref[8 * t : 8 * t + 8, g * LANES : (g + 1) * LANES] * speed
    node = node_ref[...].T
    high, low = node >> 7, node & 127
    deck = jnp.zeros((ext, height), jnp.float32)
    for g in range(groups):
        line = jnp.broadcast_to(jnp.sum(sums[g], axis=0, keepdims=True), (8, LANES))
        values = [jnp.take_along_axis(line, low[8 * q : 8 * q + 8], axis=1) for q in range(ext // 8)]
        deck = jnp.where(high == g, jnp.concatenate(values, 0), deck)
    deck = jnp.tanh(DECK_GAIN * deck)
    deck_ref[...] = deck.T
    lane = lax.broadcasted_iota(jnp.int32, (ext, height), 1)
    last_lane = lane == height - 1
    deck = deck * (2.0 * eighth) * top_ref[...]

    scale_ref[...] = jnp.broadcast_to(eighth, scale_ref.shape)
    for b in range(blocks):

        def layer(i, carry):
            at = b * ext + i
            lid = jnp.where(last_lane, pltpu.roll(deck, height - 1 - at, 1), 0.0)
            out[b, i] = base_ref[b, i] + eighth * rate_ref[b, i] - lid
            return carry

        lax.fori_loop(0, ext, layer, 0, unroll=True)


def final_kernel(dims, got, scale_ref, rim_ref, part_in, *rest):
    blocks, ext, height, bits = dims
    ghosts = rest[:bits][::-1]
    out_hbm, part, ghost, sems = rest[bits:]
    area = ext * ext
    turned = 7 - lax.broadcasted_iota(jnp.int32, (8, height), 0)
    for k in range(bits):
        for s in range(CAP):
            code = got[k * CAP + s]
            face, flip = code >> 1, code & 1

            @pl.when((code >= 0) & (flip == 0))
            def _():
                ghost[face] = ghosts[k][s]

            @pl.when((code >= 0) & (flip == 1))
            def _():
                for c in range(3):
                    for q in range(ext // 8):
                        x = ghosts[k][s, c, ext - 8 - 8 * q : ext - 8 * q, :]
                        ghost[face, c, 8 * q : 8 * q + 8, :] = jnp.take_along_axis(x, turned, axis=0)

    rows = part.reshape(blocks * area, height)
    eighth = scale_ref[0:1, 0:1]
    copies = []
    for b in range(blocks):
        for t in range(4):
            face = 4 * b + t
            side = t % 2
            near = side * (ext - 1)
            after = near + 1 - 2 * side
            g0, g1, gv = ghost[face, 0], ghost[face, 1], ghost[face, 2]
            c0, step1, behind1, u0, v1 = (rim_ref[face, q] for q in range(5))
            step0 = 0.5 * (c0 - g0)
            ghost_slope = limited(step0, 0.5 * (g0 - g1))
            slope = limited(step0, step1)
            v0 = gv + u0
            flux0 = v0 * jnp.where(v0 > 0.0, g0 + ghost_slope, c0 - slope)
            flux1 = v1 * jnp.where(v1 > 0.0, c0 + slope, behind1)
            for where, add in ((near, eighth * (flux0 - flux1)), (after, eighth * flux1)):
                if t < 2:
                    part[b, where] = part[b, where] + add
                else:
                    line = pl.ds(b * area + where, ext, stride=ext)
                    rows[line, :] = rows[line, :] + add
        copy = pltpu.make_async_copy(part.at[b], out_hbm.at[b], sems.at[b])
        copy.start()
        copies.append(copy)
    for copy in copies:
        copy.wait()


def in_hbm(x):
    return pltpu.with_memory_space_constraint(x, pltpu.HBM)


def local(fraction, fraction_start, velocity, interface_flags, block_links, deck_node, mode_shapes, mobility):
    blocks, ext, _, height = fraction.shape
    devices = lax.axis_size("family")
    bits = devices.bit_length() - 1
    modes, nodes = mode_shapes.shape
    faces = 4 * blocks
    dims = (blocks, ext, height, bits)
    f32 = jnp.float32
    vmem = pl.BlockSpec(memory_space=pltpu.VMEM)
    smem = pl.BlockSpec(memory_space=pltpu.SMEM)
    hbm = pl.BlockSpec(memory_space=pltpu.HBM)
    params = pltpu.CompilerParams(vmem_limit_bytes=24 * MIB)
    flat_node = deck_node.reshape(blocks * ext, ext)
    tables = [jnp.asarray(x, jnp.bfloat16) for x in shift_tables(height)]
    red, fill, vel = pl.pallas_call(
        functools.partial(reduce_kernel, dims),
        out_shape=[pltpu.VMEM((8, LANES), f32), pltpu.VMEM(fraction.shape, f32), pltpu.VMEM(velocity.shape, jnp.bfloat16)],
        in_specs=[hbm] * 4,
        out_specs=[vmem] * 3,
        scratch_shapes=[
            pltpu.VMEM((2 * nodes // LANES, ext * height), jnp.bfloat16),
            pltpu.VMEM((LANES, ext * height), jnp.bfloat16),
            pltpu.VMEM((blocks * ext, ext), jnp.int32),
            pltpu.VMEM((modes, nodes), f32),
            pltpu.SemaphoreType.DMA((2, blocks)),
            pltpu.SemaphoreType.DMA((2,)),
        ],
        compiler_params=params,
        name="reduce",
    )(*(in_hbm(x) for x in (flat_node, mode_shapes, fraction, velocity)))
    packed = pl.pallas_call(
        functools.partial(pack_kernel, dims, modes // 8),
        out_shape=[pltpu.VMEM((CAP, 3, ext, height), f32)] * bits + [pltpu.SMEM((bits * CAP,), jnp.int32), pltpu.VMEM((8, LANES), f32)],
        in_specs=[smem, vmem, vmem],
        out_specs=[vmem] * bits + [smem, vmem],
        scratch_shapes=[
            pltpu.VMEM((blocks * 2 * ext * 8, height), f32),
            pltpu.SMEM((bits,), jnp.int32),
            pltpu.SMEM((bits,), jnp.int32),
            pltpu.SMEM((bits * CAP,), jnp.int32),
        ],
        compiler_params=params,
        cost_estimate=pl.CostEstimate(flops=0, bytes_accessed=2 * MIB, transcendentals=0),
        name="pack",
    )(jnp.transpose(block_links, (2, 0, 1)), fill, vel)
    outgoing, (got, top_at) = packed[:bits], packed[bits:]
    received = [crossed(outgoing[k], "family", 1 << k) for k in range(bits)]
    marks = [(lax.broadcasted_iota(jnp.int32, red.shape, 1) == modes // 8).astype(f32)] * bits
    marks[1] = top_at
    order = [0, 3, 2, 1] if bits == 4 else list(range(bits))
    for q, k in enumerate(order):
        other = crossed(red, "family", 1 << k)
        red = jnp.where(marks[q] > 0.0, jnp.maximum(red, other), red + other)
    base, rate, rim, top = pl.pallas_call(
        functools.partial(rates_kernel, dims),
        out_shape=[
            jax.ShapeDtypeStruct(fraction.shape, f32),
            jax.ShapeDtypeStruct(fraction.shape, f32),
            jax.ShapeDtypeStruct((faces, 5, ext, height), f32),
            jax.ShapeDtypeStruct((ext, height), f32),
        ],
        in_specs=[vmem] * 6,
        out_specs=[vmem] * 4,
        scratch_shapes=[
            pltpu.VMEM((2 * ext * 8, height), f32),
            pltpu.VMEM((ext, ext, height), f32),
        ],
        compiler_params=params,
        cost_estimate=pl.CostEstimate(flops=80 * fraction.size, bytes_accessed=RATES_BYTES, transcendentals=0),
        name="rates",
    )(*tables, fill, vel, fraction_start, interface_flags)
    part, deck, step = pl.pallas_call(
        functools.partial(update_kernel, dims, devices),
        out_shape=[
            pltpu.VMEM(fraction.shape, f32),
            jax.ShapeDtypeStruct((blocks * ext, ext), f32),
            pltpu.VMEM((8, LANES), f32),
        ],
        in_specs=[vmem] * 7,
        out_specs=[vmem] * 3,
        compiler_params=params,
        name="update",
    )(mobility.reshape(1, modes), flat_node, mode_shapes, red, base, rate, top)
    updated, _ = pl.pallas_call(
        functools.partial(final_kernel, dims),
        out_shape=[jax.ShapeDtypeStruct(fraction.shape, f32), pltpu.VMEM(fraction.shape, f32)],
        in_specs=[smem] + [vmem] * (3 + bits),
        out_specs=[hbm, vmem],
        scratch_shapes=[
            pltpu.VMEM((faces, 3, ext, height), f32),
            pltpu.SemaphoreType.DMA((blocks,)),
        ],
        input_output_aliases={3: 1},
        compiler_params=params,
        name="finish",
    )(got, step, rim, part, *received[::-1])
    return updated, deck.reshape(blocks, ext, ext)


def solution(mesh):
    in_specs = (
        P(("groups", "family"), None, None, None),
        P(("groups", "family"), None, None, None),
        P(("groups", "family"), None, None, None, None),
        P(("groups", "family"), None, None, None),
        P("family", None, None),
        P("family", None, None),
        P(),
        P(),
    )
    out_specs = (P(("groups", "family"), None, None, None), P(("groups", "family"), None, None))
    return jax.shard_map(local, mesh=mesh, in_specs=in_specs, out_specs=out_specs, check_vma=False)
```

```python
import functools
import math

import jax
import jax.numpy as jnp
import numpy as np
from jax import lax
from jax.experimental import pallas as pl
from jax.experimental.pallas import tpu as pltpu
from jax.sharding import PartitionSpec as P

CAP = 4
CFL_NUMBER = 0.4
SHARPEN = 2.0
DECK_GAIN = 0.15
EPSILON = 1e-06
LANES = 128
MIB = 1024 * 1024
RATES_BYTES = 10 * MIB


def crossed(x, axis, mask):
    return lax.ppermute(x, axis, [(i, i ^ mask) for i in range(lax.axis_size(axis))])


def limited(first, second):
    return jnp.maximum(jnp.minimum(second, jnp.maximum(first, 0.0)), jnp.minimum(first, 0.0))


def set_bits(x):
    x = x - ((x >> 1) & 0x5555)
    x = (x & 0x3333) + ((x >> 2) & 0x3333)
    x = (x + (x >> 4)) & 0x0F0F
    return (x + (x >> 8)) & 0x1F


def route(links, me, blocks, bits, count, mask, sent, got):
    for k in range(bits):
        count[k] = 0
        mask[k] = 0
        for s in range(CAP):
            sent[k * CAP + s] = 0
            got[k * CAP + s] = -1
    shift = blocks.bit_length() - 1
    found = []
    for face in range(4 * blocks):
        b, t = face // 4, face % 4
        partner = links[0, b, t]
        differ = (partner >> shift) ^ me
        k = jnp.int32(0)
        for q in range(1, bits):
            k = k + (differ >= (1 << q)).astype(jnp.int32)
        r = count[k]
        count[k] = r + 1
        sent[k * CAP + r] = face
        source = (partner & (blocks - 1)) * 4 + links[1, b, t]
        mask[k] = mask[k] | (jnp.int32(1) << source)
        found.append((k, source))
    for face, (k, source) in enumerate(found):
        rank = set_bits(mask[k] & ((jnp.int32(1) << source) - 1))
        got[k * CAP + rank] = 2 * face + links[2, face // 4, face % 4]


def pack_kernel(dims, tiles, sent, fill, vel, *rest):
    blocks, ext, height, bits = dims
    outs = rest[:bits]
    top_at, edge = rest[bits:]
    top_at[...] = (lax.broadcasted_iota(jnp.int32, top_at.shape, 1) == tiles).astype(jnp.float32)
    area = ext * ext
    for b in range(blocks):
        for side in range(2):
            x = vel[b, 1, :, side * (ext - 16) : side * (ext - 16) + 16, :].astype(jnp.float32)[:, 8 * side : 8 * side + 8]
            edge[pl.ds((b * 2 + side) * ext * 8, ext * 8), :] = x.reshape(ext * 8, height)
    rows = fill.reshape(blocks * area, height)
    for k in range(bits):
        for s in range(CAP):
            face = sent[k * CAP + s]
            b, t = face >> 2, face & 3
            side = t & 1
            sign = (2 * side - 1).astype(jnp.float32)
            near = side * (ext - 1)
            after = near + 1 - 2 * side

            @pl.when(t < 2)
            def _():
                outs[k][s, 0] = fill[b, near]
                outs[k][s, 1] = fill[b, after]
                outs[k][s, 2] = vel[b, 0, near].astype(jnp.float32) * sign

            @pl.when(t >= 2)
            def _():
                outs[k][s, 0] = rows[pl.ds(b * area + near, ext, stride=ext), :]
                outs[k][s, 1] = rows[pl.ds(b * area + after, ext, stride=ext), :]
                outs[k][s, 2] = edge[pl.ds((b * 2 + side) * ext * 8 + side * 7, ext, stride=8), :] * sign


def route_kernel(dims, tiles, links, sent, got, top_at, count, mask):
    blocks, ext, height, bits = dims
    top_at[...] = (lax.broadcasted_iota(jnp.int32, top_at.shape, 1) == tiles).astype(jnp.float32)
    route(links, lax.axis_index("family"), blocks, bits, count, mask, sent, got)


def reduce_kernel(dims, node_hbm, shapes_hbm, fill_hbm, vel_hbm, red_ref, fill, vel, left, right, node_ref, shapes_ref, sems, late):
    blocks, ext, height, bits = dims
    early = pltpu.make_async_copy(node_hbm, node_ref, late.at[0])
    early.start()
    fill_copies, vel_copies = [], []
    for b in range(blocks):
        fill_copies.append(pltpu.make_async_copy(fill_hbm.at[b], fill.at[b], sems.at[0, b]))
        vel_copies.append(pltpu.make_async_copy(vel_hbm.at[b], vel.at[b], sems.at[1, b]))
        vel_copies[b].start()
        fill_copies[b].start()
    last = pltpu.make_async_copy(shapes_hbm, shapes_ref, late.at[1])
    last.start()
    early.wait()
    node = node_ref[...].T
    high, low = node >> 7, node & 127
    low_at = lax.broadcasted_iota(jnp.int32, (LANES, height), 0)
    for j in range(ext):
        right[:, j * height : (j + 1) * height] = jnp.where(low_at == low[j : j + 1], 1.0, 0.0).astype(jnp.bfloat16)
    lane = lax.broadcasted_iota(jnp.int32, (ext, height), 1)
    pressure = jnp.zeros((ext, height), jnp.float32)
    speed = jnp.zeros((ext, height), jnp.bfloat16)
    for b in range(blocks):
        vel_copies[b].wait()
        fill_copies[b].wait()

        def step(i, carry):
            pressure, speed = carry
            up = vel[b, 2, i]
            speed = jnp.maximum(speed, jnp.abs(vel[b, 0, i]))
            speed = jnp.maximum(speed, jnp.abs(vel[b, 1, i]))
            speed = jnp.maximum(speed, jnp.abs(up))
            up = up.astype(jnp.float32)
            push = fill[b, i] * (1.0 + up * up)
            at = b * ext + i
            pressure = jnp.where(lane == at, pltpu.roll(push, at + 1, 1), pressure)
            return pressure, speed

        pressure, speed = lax.fori_loop(0, ext, step, (pressure, speed), unroll=True)
    last.wait()
    groups = shapes_ref.shape[1] // LANES
    first = pressure.astype(jnp.bfloat16).astype(jnp.float32)
    second = pressure - first
    high_at = lax.broadcasted_iota(jnp.int32, (groups, height), 0)
    for j in range(ext):
        same = high_at == high[j : j + 1]
        cols = pl.ds(j * height, height)
        left[0:groups, cols] = jnp.where(same, first[j : j + 1], 0.0).astype(jnp.bfloat16)
        left[groups : 2 * groups, cols] = jnp.where(same, second[j : j + 1], 0.0).astype(jnp.bfloat16)
    nodal = lax.dot_general(left[...], right[...], (((1,), (1,)), ((), ())), preferred_element_type=jnp.float32)
    nodal = nodal[:groups] + nodal[groups:]
    lane8 = lax.broadcasted_iota(jnp.int32, (8, LANES), 1)
    tiles = shapes_ref.shape[0] // 8
    top = jnp.max(jnp.max(speed.astype(jnp.float32), axis=0, keepdims=True), axis=1, keepdims=True)
    red = jnp.where(lane8 == tiles, top, 0.0)
    for t in range(tiles):
        total = jnp.zeros((8, LANES), jnp.float32)
        for g in range(groups):
            total = total + shapes_ref[8 * t : 8 * t + 8, g * LANES : (g + 1) * LANES] * nodal[g : g + 1]
        red = jnp.where(lane8 == t, jnp.sum(total, axis=1, keepdims=True), red)
    red_ref[...] = red


def shift_tables(height):
    k = np.arange(height)
    eye = np.eye(height, dtype=np.float32)
    nxt = np.eye(height, k=-1, dtype=np.float32)
    nxt2 = np.eye(height, k=-2, dtype=np.float32)
    prv = np.eye(height, k=1, dtype=np.float32)
    before = 0.5 * (eye - prv); before[:, 0] = 0
    step = 0.5 * (nxt - eye); step[:, -1] = 0
    after = 0.5 * (nxt2 - nxt); after[:, -2:] = 0
    cells = np.concatenate([before, step, after, nxt], 1)
    flow = nxt + eye; flow[:, -1] = 0
    return np.concatenate([cells, cells], 0), flow
def column_kernel(dims, tiles, cells_ref, flow_ref, fill, vel, lift, top_at):
    blocks, ext, height, bits = dims
    top_at[...] = (lax.broadcasted_iota(jnp.int32, top_at.shape, 1) == tiles).astype(jnp.float32)
    layers = 8
    size = layers * ext

    def block(b, carry):
        for c in range(ext // layers):
            part = pl.ds(c * layers, layers)
            x = fill[b, part].reshape(size, height)
            u = vel[b, 2, part].reshape(size, height)
            high = x.astype(jnp.bfloat16)
            low = (x - high.astype(jnp.float32)).astype(jnp.bfloat16)
            y = jnp.dot(jnp.concatenate([high, low], 1), cells_ref[...], preferred_element_type=jnp.float32)
            v = jnp.dot(u, flow_ref[...], preferred_element_type=jnp.float32)
            step = y[:, height : 2 * height]
            ahead = x + limited(step, y[:, :height])
            behind = y[:, 3 * height :] - limited(step, y[:, 2 * height : 3 * height])
            lift[b, part] = (v * jnp.where(v > 0.0, ahead, behind)).reshape(layers, ext, height)
        return carry

    lax.fori_loop(0, blocks, block, 0)


def rates_kernel(dims, fill, vel, lift, start, flag, base_ref, rate_ref, rim_ref, top_ref, edge):
    blocks, ext, height, bits = dims
    area = ext * ext
    lane = lax.broadcasted_iota(jnp.int32, (ext, height), 1)
    row = lax.broadcasted_iota(jnp.int32, (ext, height), 0)
    open_row = (row >= 1) & (row <= ext - 3)
    rows = fill.reshape(blocks * area, height)
    top = jnp.zeros((ext, height), jnp.float32)
    def block(b, top):

        def own(i, f, h):
            flux = lift[b, i]
            rate = pltpu.roll(flux, 1, 1) - flux
            step = pltpu.roll(h, ext - 1, 0) - h
            slope = limited(pltpu.roll(step, 1, 0), step)
            u = vel[b, 1, i].astype(jnp.float32)
            v = u + pltpu.roll(u, ext - 1, 0)
            v = jnp.where(open_row, v, 0.0)
            flux = v * jnp.where(v > 0.0, f + slope, pltpu.roll(f - slope, ext - 1, 0))
            rate = rate + (pltpu.roll(flux, 1, 0) - flux)
            sharp = (f * (1.0 - f)) * ((4.0 * SHARPEN) * f - 2.0 * SHARPEN)
            rate = rate + jnp.where(flag[b, i] != 0, sharp, 0.0)
            base_ref[b, i] = 0.75 * start[b, i] + 0.25 * f
            return rate

        def picked(i, f, top):
            at = b * ext + i
            return jnp.where(lane == at, pltpu.roll(f, at + 1, 1), top)

        f0 = fill[b, 0]
        rate_ref[b, 0] = own(0, f0, 0.5 * f0)
        top = picked(0, f0, top)
        f1 = fill[b, 1]
        h1 = 0.5 * f1
        rate1 = own(1, f1, h1)
        top = picked(1, f1, top)
        f2 = fill[b, 2]
        h2 = 0.5 * f2
        step = h2 - h1
        ahead = f1 + limited(h1 - 0.5 * f0, step)

        def layer(i, carry):
            f, h, step_before, ahead, flux_before, u_before, rate_before, top = carry
            f_next = fill[b, i + 1]
            h_next = 0.5 * f_next
            step = h_next - h
            slope = limited(step_before, step)
            u = vel[b, 0, i].astype(jnp.float32)
            v = u_before + u
            flux = v * jnp.where(v > 0.0, ahead, f - slope)
            rate_ref[b, i - 1] = rate_before + (flux_before - flux)
            return f_next, h_next, step, f + slope, flux, u, own(i, f, h), picked(i, f, top)

        carry = (f2, h2, step, ahead, jnp.zeros_like(f0), vel[b, 0, 1].astype(jnp.float32), rate1, top)
        carry = lax.fori_loop(2, ext - 1, layer, carry, unroll=True)
        f, h, _, _, flux, _, rate, top = carry
        rate_ref[b, ext - 2] = rate + flux
        rate_ref[b, ext - 1] = own(ext - 1, f, h)
        top = picked(ext - 1, f, top)

        for side in range(2):
            x = vel[b, 1, :, side * (ext - 16) : side * (ext - 16) + 16, :].astype(jnp.float32)[:, 8 * side : 8 * side + 8]
            edge[pl.ds(side * ext * 8, ext * 8), :] = x.reshape(ext * 8, height)
        for t in range(4):
            side = t % 2
            sign = 1.0 - 2.0 * side
            at = [side * (ext - 1) + d * (1 - 2 * side) for d in range(3)]
            if t < 2:
                cells = [fill[b, i] for i in at]
                flows = [vel[b, 0, i].astype(jnp.float32) * sign for i in at[:2]]
            else:
                cells = [rows[pl.ds(b * area + j, ext, stride=ext), :] for j in at]
                flows = [edge[pl.ds(side * ext * 8 + j % 8, ext, stride=8), :] * sign for j in at[:2]]
            step = 0.5 * (cells[1] - cells[0])
            slope = limited(step, 0.5 * (cells[2] - cells[1]))
            rim_ref[4 * b + t, 0] = cells[0]
            rim_ref[4 * b + t, 1] = step
            rim_ref[4 * b + t, 2] = cells[1] - slope
            rim_ref[4 * b + t, 3] = flows[0]
            rim_ref[4 * b + t, 4] = flows[0] + flows[1]
        return top
    top_ref[...] = lax.fori_loop(0, blocks, block, top)


def update_kernel(dims, devices, mobility_ref, node_ref, shapes_ref, red_ref, base_ref, rate_ref, top_ref, out, deck_ref, scale_ref):
    blocks, ext, height, bits = dims
    area = ext * ext
    tiles = shapes_ref.shape[0] // 8
    groups = shapes_ref.shape[1] // LANES
    red = red_ref[...]
    time_step = CFL_NUMBER / (red[0:1, tiles : tiles + 1] + EPSILON)
    eighth = 0.125 * time_step
    scale = math.sqrt(shapes_ref.shape[1]) / (blocks * devices * area)
    lane8 = lax.broadcasted_iota(jnp.int32, (8, LANES), 1)
    sub8 = lax.broadcasted_iota(jnp.int32, (8, LANES), 0)
    mobility = mobility_ref[...]
    sums = [jnp.zeros((8, LANES), jnp.float32) for _ in range(groups)]
    width = mobility.shape[1]
    for t in range(tiles):
        pick = lax.broadcasted_iota(jnp.int32, (8, width), 1) == 8 * t + lax.broadcasted_iota(jnp.int32, (8, width), 0)
        gain = jnp.sum(jnp.where(pick, mobility, 0.0), axis=1, keepdims=True)
        speed = jnp.broadcast_to(gain * (red[:, t : t + 1] * scale), (8, LANES))
        for g in range(groups):
            sums[g] = sums[g] + shapes_ref[8 * t : 8 * t + 8, g * LANES : (g + 1) * LANES] * speed
    node = node_ref[...].T
    high, low = node >> 7, node & 127
    deck = jnp.zeros((ext, height), jnp.float32)
    for g in range(groups):
        line = jnp.broadcast_to(jnp.sum(sums[g], axis=0, keepdims=True), (8, LANES))
        values = [jnp.take_along_axis(line, low[8 * q : 8 * q + 8], axis=1) for q in range(ext // 8)]
        deck = jnp.where(high == g, jnp.concatenate(values, 0), deck)
    deck = jnp.tanh(DECK_GAIN * deck)
    deck_ref[...] = deck.T
    lane = lax.broadcasted_iota(jnp.int32, (ext, height), 1)
    last_lane = lane == height - 1
    deck = deck * (2.0 * eighth) * top_ref[...]

    scale_ref[...] = jnp.broadcast_to(eighth, scale_ref.shape)
    for b in range(blocks):

        def layer(i, carry):
            at = b * ext + i
            lid = jnp.where(last_lane, pltpu.roll(deck, height - 1 - at, 1), 0.0)
            out[b, i] = base_ref[b, i] + eighth * rate_ref[b, i] - lid
            return carry

        lax.fori_loop(0, ext, layer, 0, unroll=True)


def final_kernel(dims, got, scale_ref, rim_ref, part_in, *rest):
    blocks, ext, height, bits = dims
    ghosts = rest[:bits][::-1]
    out_hbm, part, ghost, sems = rest[bits:]
    area = ext * ext
    turned = 7 - lax.broadcasted_iota(jnp.int32, (8, height), 0)
    for k in range(bits):
        for s in range(CAP):
            code = got[k * CAP + s]
            face, flip = code >> 1, code & 1

            @pl.when((code >= 0) & (flip == 0))
            def _():
                ghost[face] = ghosts[k][s]

            @pl.when((code >= 0) & (flip == 1))
            def _():
                for c in range(3):
                    for q in range(ext // 8):
                        x = ghosts[k][s, c, ext - 8 - 8 * q : ext - 8 * q, :]
                        ghost[face, c, 8 * q : 8 * q + 8, :] = jnp.take_along_axis(x, turned, axis=0)

    rows = part.reshape(blocks * area, height)
    eighth = scale_ref[0:1, 0:1]
    copies = []
    for b in range(blocks):
        for t in range(4):
            face = 4 * b + t
            side = t % 2
            near = side * (ext - 1)
            after = near + 1 - 2 * side
            g0, g1, gv = ghost[face, 0], ghost[face, 1], ghost[face, 2]
            c0, step1, behind1, u0, v1 = (rim_ref[face, q] for q in range(5))
            step0 = 0.5 * (c0 - g0)
            ghost_slope = limited(step0, 0.5 * (g0 - g1))
            slope = limited(step0, step1)
            v0 = gv + u0
            flux0 = v0 * jnp.where(v0 > 0.0, g0 + ghost_slope, c0 - slope)
            flux1 = v1 * jnp.where(v1 > 0.0, c0 + slope, behind1)
            for where, add in ((near, eighth * (flux0 - flux1)), (after, eighth * flux1)):
                if t < 2:
                    part[b, where] = part[b, where] + add
                else:
                    line = pl.ds(b * area + where, ext, stride=ext)
                    rows[line, :] = rows[line, :] + add
        copy = pltpu.make_async_copy(part.at[b], out_hbm.at[b], sems.at[b])
        copy.start()
        copies.append(copy)
    for copy in copies:
        copy.wait()


def in_hbm(x):
    return pltpu.with_memory_space_constraint(x, pltpu.HBM)


def local(fraction, fraction_start, velocity, interface_flags, block_links, deck_node, mode_shapes, mobility):
    blocks, ext, _, height = fraction.shape
    devices = lax.axis_size("family")
    bits = devices.bit_length() - 1
    modes, nodes = mode_shapes.shape
    faces = 4 * blocks
    dims = (blocks, ext, height, bits)
    f32 = jnp.float32
    vmem = pl.BlockSpec(memory_space=pltpu.VMEM)
    smem = pl.BlockSpec(memory_space=pltpu.SMEM)
    hbm = pl.BlockSpec(memory_space=pltpu.HBM)
    params = pltpu.CompilerParams(vmem_limit_bytes=24 * MIB)
    flat_node = deck_node.reshape(blocks * ext, ext)
    tables = [jnp.asarray(x, jnp.bfloat16) for x in shift_tables(height)]
    red, fill, vel = pl.pallas_call(
        functools.partial(reduce_kernel, dims),
        out_shape=[
            pltpu.VMEM((8, LANES), f32),
            pltpu.VMEM(fraction.shape, f32),
            pltpu.VMEM(velocity.shape, jnp.bfloat16),
        ],
        in_specs=[hbm] * 4,
        out_specs=[vmem] * 3,
        scratch_shapes=[
            pltpu.VMEM((2 * nodes // LANES, ext * height), jnp.bfloat16),
            pltpu.VMEM((LANES, ext * height), jnp.bfloat16),
            pltpu.VMEM((blocks * ext, ext), jnp.int32),
            pltpu.VMEM((modes, nodes), f32),
            pltpu.SemaphoreType.DMA((2, blocks)),
            pltpu.SemaphoreType.DMA((2,)),
        ],
        compiler_params=params,
        name="reduce",
    )(*(in_hbm(x) for x in (flat_node, mode_shapes, fraction, velocity)))
    sent, got, routed_at = pl.pallas_call(
        functools.partial(route_kernel, dims, modes // 8),
        out_shape=[
            pltpu.SMEM((bits * CAP,), jnp.int32),
            pltpu.SMEM((bits * CAP,), jnp.int32),
            pltpu.VMEM((8, LANES), f32),
        ],
        in_specs=[smem],
        out_specs=[smem, smem, vmem],
        scratch_shapes=[pltpu.SMEM((bits,), jnp.int32), pltpu.SMEM((bits,), jnp.int32)],
        compiler_params=params,
        name="route",
    )(jnp.transpose(block_links, (2, 0, 1)))
    packed = pl.pallas_call(
        functools.partial(pack_kernel, dims, modes // 8),
        out_shape=[pltpu.VMEM((CAP, 3, ext, height), f32)] * bits + [pltpu.VMEM((8, LANES), f32)],
        in_specs=[smem, vmem, vmem],
        out_specs=[vmem] * bits + [vmem],
        scratch_shapes=[
            pltpu.VMEM((blocks * 2 * ext * 8, height), f32),
        ],
        compiler_params=params,
        cost_estimate=pl.CostEstimate(flops=0, bytes_accessed=2 * MIB, transcendentals=0),
        name="pack",
    )(sent, fill, vel)
    outgoing, top_at = packed[:bits], packed[bits]
    received = [crossed(outgoing[k], "family", 1 << k) for k in range(bits)]
    marks = [(lax.broadcasted_iota(jnp.int32, red.shape, 1) == modes // 8).astype(f32)] * bits
    lift, lift_at = pl.pallas_call(
        functools.partial(column_kernel, dims, modes // 8),
        out_shape=[pltpu.VMEM(fraction.shape, f32), pltpu.VMEM((8, LANES), f32)],
        in_specs=[vmem] * 4,
        out_specs=[vmem] * 2,
        compiler_params=params,
        cost_estimate=pl.CostEstimate(flops=0, bytes_accessed=2 * MIB, transcendentals=0),
        name="column",
    )(*tables, fill, vel)
    marks[0], marks[1], marks[2] = routed_at, top_at, lift_at
    order = [0, 3, 1, 2] if bits == 4 else list(range(bits))
    for q, k in enumerate(order):
        other = crossed(red, "family", 1 << k)
        red = jnp.where(marks[q] > 0.0, jnp.maximum(red, other), red + other)
    base, rate, rim, top = pl.pallas_call(
        functools.partial(rates_kernel, dims),
        out_shape=[
            jax.ShapeDtypeStruct(fraction.shape, f32),
            jax.ShapeDtypeStruct(fraction.shape, f32),
            jax.ShapeDtypeStruct((faces, 5, ext, height), f32),
            jax.ShapeDtypeStruct((ext, height), f32),
        ],
        in_specs=[vmem] * 5,
        out_specs=[vmem] * 4,
        scratch_shapes=[pltpu.VMEM((2 * ext * 8, height), f32)],
        compiler_params=params,
        cost_estimate=pl.CostEstimate(flops=80 * fraction.size, bytes_accessed=RATES_BYTES, transcendentals=0),
        name="rates",
    )(fill, vel, lift, fraction_start, interface_flags)
    part, deck, step = pl.pallas_call(
        functools.partial(update_kernel, dims, devices),
        out_shape=[
            pltpu.VMEM(fraction.shape, f32),
            jax.ShapeDtypeStruct((blocks * ext, ext), f32),
            pltpu.VMEM((8, LANES), f32),
        ],
        in_specs=[vmem] * 7,
        out_specs=[vmem] * 3,
        compiler_params=params,
        name="update",
    )(mobility.reshape(1, modes), flat_node, mode_shapes, red, base, rate, top)
    updated, _ = pl.pallas_call(
        functools.partial(final_kernel, dims),
        out_shape=[jax.ShapeDtypeStruct(fraction.shape, f32), pltpu.VMEM(fraction.shape, f32)],
        in_specs=[smem] + [vmem] * (3 + bits),
        out_specs=[hbm, vmem],
        scratch_shapes=[
            pltpu.VMEM((faces, 3, ext, height), f32),
            pltpu.SemaphoreType.DMA((blocks,)),
        ],
        input_output_aliases={3: 1},
        compiler_params=params,
        name="finish",
    )(got, step, rim, part, *received[::-1])
    return updated, deck.reshape(blocks, ext, ext)


def solution(mesh):
    in_specs = (
        P(("groups", "family"), None, None, None),
        P(("groups", "family"), None, None, None),
        P(("groups", "family"), None, None, None, None),
        P(("groups", "family"), None, None, None),
        P("family", None, None),
        P("family", None, None),
        P(),
        P(),
    )
    out_specs = (P(("groups", "family"), None, None, None), P(("groups", "family"), None, None))
    return jax.shard_map(local, mesh=mesh, in_specs=in_specs, out_specs=out_specs, check_vma=False)
```
